32 devices in a mesh: dp: 8 (over z, core), tensor: 4 (over y, x).
Axes of the slice: x: 2, y: 2, z: 4, core: 2. Of those that a mesh axis runs over, the one named last changes fastest.
Arguments:
- queries: bfloat16 [1024, 8192], P('dp', 'tensor'), parts along dimension 0
- tree_states: bfloat16 [1024, 2048], P(('dp', 'tensor')), parts along dimension 0, may hold values from -6 to 6
- cache_codes: bfloat16 [640, 8, 2, 64, 128], P(('dp', 'tensor')), parts along dimension 0, may hold values from 0 to 255, as said below
- cache_scales: float32 [640, 8, 2, 128], P(('dp', 'tensor')), parts along dimension 0, may hold values from 0.3 to 3
- bit_widths: int32 [64], P('dp'), parts along dimension 0, may hold values from 2 to 8, as said below
- page_table: int32 [32, 20], P('dp'), parts along dimension 0, may hold values from 0 to 19, as said below
- lengths: int32 [32], P('dp'), parts along dimension 0, may hold values from 1 to 1280, as said below
- parents: int32 [32, 32], P('dp'), parts along dimension 0, may hold values from 0 to 30, as said below
- tree_mask: int32 [32, 32, 32], P('dp'), parts along dimension 0, may hold values from 0 to 1, as said below
- output_weight: bfloat16 [8192, 8192], P('tensor'), may hold values from -0.09375 to 0.09375
- residual: bfloat16 [1024, 8192], P('dp', 'tensor'), parts along dimension 0
- norm_gain: bfloat16 [8192], P('tensor'), may hold values from 0.099609375 to 1.8984375
- draft_weight: bfloat16 [8192, 2048], P('tensor'), may hold values from -0.09375 to 0.09375
Outputs:
- feature: bfloat16 [1024, 8192], P('dp', 'tensor'), parts along dimension 0
- draft_projection: bfloat16 [1024, 2048], P('dp', 'tensor'), parts along dimension 0
The draws below stay inside these ranges and needn't reach their ends.
There are 8 independent parts, one for each index of `dp`. The reference program is written for one: setup_inputs(seed, part) draws one part's arguments, and reference() takes and returns one part's arrays. A program takes and returns all parts, laid end to end along the dimension named above; an argument that names none is the same for every part. Nothing has to cross between parts.
Inputs may be any that keep to these rules, and one draw needn't show every extreme that they name: `bit_widths`: every head holds 2, 4 or 8 bits. `cache_codes`: on KV head g every entry is a whole number from 0 to 2 to the power bit_widths[g], minus 1. `page_table`: for each c, the entries of columns c * 5 to (c + 1) * 5 - 1 over all requests form a permutation of 0 to 19: slots in the pool of tensor index c. `lengths`: some request of every part has exactly 1280 positions. parents[r, 0] = 0; for i > 0 the parent is below i, in node i's own block of 8 nodes, or in the first block when i is the first node of its block. tree_mask[r, i, j] = 1 exactly when j is i or an ancestor of i under parents.
All inputs are finite; a program needn't handle non-finite values.
Results may differ from the reference program's by a relative error of at most 0.012.
Values may be sent and summed in bfloat16 or wider, within the bound.
A program may use at most 128 MiB of HBM per device.

```python
import math
import jax
import jax.numpy as jnp
import numpy as np
from jax import lax

D = 8192
HQ = 64
KVH = 8
HD = 128
NODES = 32
TBLOCK = 8
PAGE = 64
PAGES_DEV = 5
REQS = 4
CTX = 1280
POOL = 20
ROWS = 128
N_TENSOR = 4


def bit_helper(key, part):
    combos = 3 ** KVH
    offset = jax.random.randint(jax.random.fold_in(key, 11), (), 0, combos, dtype=jnp.int32)
    number = (offset + jnp.asarray(part, jnp.int32)) % combos
    powers = jnp.asarray(np.power(3, np.arange(KVH)).astype(np.int32))
    digits = number // powers % 3
    return jnp.left_shift(jnp.int32(2), digits.astype(jnp.int32)).astype(jnp.int32)


def draw_bit_widths(key, part):
    return bit_helper(key, part)


def draw_cache_codes(key, part):
    widths = bit_helper(key, part)
    ceiling = jnp.left_shift(jnp.int32(1), widths)[None, :, None, None, None]
    levels_drawn = jax.random.randint(jax.random.fold_in(key, 12), (N_TENSOR * POOL, KVH, 2, PAGE, HD), 0, ceiling, dtype=jnp.int32)
    return levels_drawn.astype(jnp.float32).astype(jnp.bfloat16)


def one_permutation(device_key):
    return jax.random.permutation(device_key, POOL)


def draw_page_table(key, part):
    device_keys = jax.random.split(jax.random.fold_in(key, 21), N_TENSOR)
    shuffled = jax.vmap(one_permutation)(device_keys)
    arranged = shuffled.reshape(N_TENSOR, REQS, PAGES_DEV).transpose(1, 0, 2)
    return arranged.reshape(REQS, N_TENSOR * PAGES_DEV).astype(jnp.int32)


def draw_lengths(key, part):
    drawn = jax.random.randint(jax.random.fold_in(key, 31), (REQS,), 1, CTX + 1, dtype=jnp.int32)
    chosen = jax.random.randint(jax.random.fold_in(key, 32), (), 0, REQS, dtype=jnp.int32)
    return jnp.where(jnp.arange(REQS, dtype=jnp.int32) == chosen, CTX, drawn).astype(jnp.int32)


def tree_helper(key):
    node_ids = jnp.arange(NODES, dtype=jnp.int32)
    block_first = node_ids % TBLOCK == 0
    lowest = jnp.where(block_first, 0, node_ids // TBLOCK * TBLOCK)
    highest = jnp.where(node_ids == 0, 1, jnp.where(block_first, TBLOCK, node_ids))
    parent = jax.random.randint(jax.random.fold_in(key, 41), (REQS, NODES), lowest[None, :], highest[None, :], dtype=jnp.int32)
    parent = jnp.where(node_ids[None, :] == 0, 0, parent).astype(jnp.int32)
    last_node = (node_ids[None, :] == NODES - 1) & (jnp.arange(REQS, dtype=jnp.int32)[:, None] == 0)
    parent = jnp.where(last_node, NODES - 2, parent).astype(jnp.int32)

    def closure(parent_row):

        def add_node(lineage_rows, node):
            ancestors = jnp.where(node > 0, lineage_rows[parent_row[node]], jnp.zeros((NODES,), jnp.int32))
            lineage = jnp.maximum(ancestors, (node_ids == node).astype(jnp.int32))
            return (lineage_rows.at[node].set(lineage), None)
        result, unused = lax.scan(add_node, jnp.zeros((NODES, NODES), jnp.int32), node_ids)
        return result
    return (parent, jax.vmap(closure)(parent))


def draw_parents(key, part):
    parent, lineage = tree_helper(key)
    return parent


def draw_tree_mask(key, part):
    parent, lineage = tree_helper(key)
    return lineage.astype(jnp.int32)


def draw_queries(key, part):
    sample_key = jax.random.fold_in(jax.random.fold_in(key, 61), 0)
    sample = 2.0 * jax.random.normal(sample_key, (ROWS, HQ, HD), jnp.float32)
    return sample.reshape(ROWS, HQ * HD).astype(jnp.bfloat16)


def draw_residual(key, part):
    sample_key, column_key, row_key = jax.random.split(jax.random.fold_in(key, 51), 3)
    rising = jnp.exp(jnp.log(3.0) * (jnp.arange(D, dtype=jnp.float32) / D - 0.5))
    column_scale = jnp.exp(jax.random.uniform(column_key, (D,), jnp.float32, jnp.log(0.5), jnp.log(2.0)))
    row_scale = jnp.exp(jax.random.uniform(row_key, (ROWS, 1), jnp.float32, jnp.log(0.3), jnp.log(3.0)))
    sample = jax.random.normal(sample_key, (ROWS, D), jnp.float32)
    return (sample * rising[None, :] * column_scale[None, :] * row_scale).astype(jnp.bfloat16)


def with_spikes(array, rng, source, target, parts, factor):
    owner, partner = [(jnp.arange(array.shape[axis_at]) // (array.shape[axis_at] // parts)).reshape([-1 if axis == axis_at else 1 for axis in range(array.ndim)]) for axis_at in (source, target)]
    chosen = jax.random.permutation(rng, parts)[partner]
    strong = (owner == chosen) | (owner == (partner + parts // 2) % parts)
    return jnp.where(strong, factor * array, array)


def shard_levels(key, dims, cuts, smallest, largest):
    loudness, own = 1.0, jax.random.fold_in(key, 6)
    for axis_at, shards_of in cuts:
        heights = jnp.exp(jax.random.uniform(jax.random.fold_in(own, axis_at), (shards_of,), jnp.float32, smallest / len(cuts), largest / len(cuts)))
        loudness = loudness * jnp.repeat(heights, dims[axis_at] // shards_of).reshape([-1 if axis == axis_at else 1 for axis in range(len(dims))])
    return loudness


def noise(rng, dims, deviation, most, shards=(), held_as=jnp.bfloat16):
    entries = jax.random.normal(rng, dims, jnp.float32) * deviation
    if len(shards) > 0:
        entries = shard_levels(rng, dims, shards, -0.22, 0.18) * entries
    return jnp.clip(entries, min=-most, max=most).astype(held_as)


def heavy_noise(rng, extent, deviation, bound, cuts, heavy, kind=jnp.bfloat16):
    values = deviation * jax.random.normal(rng, extent, jnp.float32)
    if cuts:
        values = values * shard_levels(rng, extent, cuts, -0.22, 0.18)
    return jnp.clip(with_spikes(values, jax.random.fold_in(rng, 3), *heavy), -bound, bound).astype(kind)


def setup_inputs(seed: int = 0, part: int = 0) -> dict:
    key_list = jax.random.split(jax.random.key(seed), 14)
    part_splits = jax.random.split(jax.random.fold_in(key_list[13], part), 14)
    return {
        "queries": draw_queries(jax.random.fold_in(jax.random.fold_in(key_list[13], part), 71), part),
        "tree_states": noise(part_splits[1], (ROWS, 2 * KVH * HD), 1.0, 6.0, ((0, 4),)),
        "cache_codes": draw_cache_codes(jax.random.fold_in(jax.random.fold_in(key_list[13], part), 71), part),
        "cache_scales": jnp.clip(jnp.exp(math.log(3.0) - 2.3025851 * jax.random.uniform(part_splits[3], (N_TENSOR * POOL, KVH, 2, HD), jnp.float32) ** shard_levels(part_splits[3], (N_TENSOR * POOL, KVH, 2, HD), ((0, 4),), -0.2, 0.2)), 0.3, 3.0),
        "bit_widths": draw_bit_widths(jax.random.fold_in(jax.random.fold_in(key_list[13], part), 71), part),
        "page_table": draw_page_table(jax.random.fold_in(jax.random.fold_in(key_list[13], part), 71), part),
        "lengths": draw_lengths(jax.random.fold_in(jax.random.fold_in(key_list[13], part), 71), part),
        "parents": draw_parents(jax.random.fold_in(jax.random.fold_in(key_list[13], part), 71), part),
        "tree_mask": draw_tree_mask(jax.random.fold_in(jax.random.fold_in(key_list[13], part), 71), part),
        "output_weight": heavy_noise(key_list[9], (HQ * HD, D), (HQ * HD) ** -0.5, 0.09375, ((0, 4),), (0, 1, 4, 2.0)),
        "residual": draw_residual(jax.random.fold_in(jax.random.fold_in(key_list[13], part), 71), part),
        "norm_gain": jnp.clip(1.0 + 0.18 * jax.random.normal(key_list[11], (D,), jnp.float32), 0.099609375, 1.8984375).astype(jnp.bfloat16),
        "draft_weight": heavy_noise(key_list[12], (D, 2 * KVH * HD), D ** -0.5, 0.09375, ((0, 4),), (0, 1, 4, 2.0)),
    }


masked_score = -1e+30
epsilon = 1e-05

def rounded(values):
    return lax.optimization_barrier(values.astype(jnp.bfloat16)).astype(jnp.float32)

def dequantize(cache_codes, cache_scales, bit_widths):
    levels = jnp.exp2(bit_widths.astype(jnp.float32))[None, :, None, None, None]
    drawn = cache_codes.astype(jnp.float32)
    scaled = cache_scales.astype(jnp.float32)[:, :, :, None, :]
    return (scaled * (2.0 * drawn - levels + 1.0) / levels).astype(jnp.bfloat16)

def block_partial(request_query, key_rows, value_rows, in_range):
    scores = jnp.einsum('nkgd,ktd->nkgt', request_query, key_rows.astype(jnp.float32)) / math.sqrt(HD)
    live = in_range[None, None, None, :]
    scores = jnp.where(live, scores, masked_score)
    block_max = lax.optimization_barrier(jnp.max(scores, axis=-1))
    weights = jnp.where(live, jnp.exp(scores - block_max[..., None]), 0.0)
    block_sum = lax.optimization_barrier(jnp.sum(weights, axis=-1))
    block_out = jnp.einsum('nkgt,ktd->nkgd', rounded(weights), value_rows.astype(jnp.float32))
    block_out = block_out / jnp.where(block_sum > 0, block_sum, 1.0)[..., None]
    return (block_max, block_sum, block_out.astype(jnp.bfloat16))

def reference(queries, tree_states, cache_codes, cache_scales, bit_widths, page_table, lengths, parents, tree_mask, output_weight, residual, norm_gain, draft_weight):
    groups = HQ // KVH
    block_span = PAGES_DEV * PAGE
    dequant = dequantize(cache_codes, cache_scales, bit_widths)
    tree_keys = tree_states[:, :KVH * HD].reshape(REQS, NODES, KVH, HD).astype(jnp.float32)
    tree_values = tree_states[:, KVH * HD:].reshape(REQS, NODES, KVH, HD).astype(jnp.float32)
    outputs = []
    for request in range(REQS):
        request_query = queries[request * NODES:(request + 1) * NODES].astype(jnp.float32).reshape(NODES, KVH, groups, HD)
        request_pages = page_table[request]
        request_length = lengths[request]

        def one_block(block_id):
            slot_ids = block_id * POOL + lax.dynamic_slice_in_dim(request_pages, block_id * PAGES_DEV, PAGES_DEV)
            chosen = jnp.take(dequant, slot_ids, axis=0)
            key_rows = chosen[:, :, 0].transpose(1, 0, 2, 3).reshape(KVH, block_span, HD)
            value_rows = chosen[:, :, 1].transpose(1, 0, 2, 3).reshape(KVH, block_span, HD)
            positions = block_id * block_span + jnp.arange(block_span, dtype=jnp.int32)
            return block_partial(request_query, key_rows, value_rows, positions < request_length)
        maxima, sums, partial_out = lax.map(one_block, jnp.arange(N_TENSOR, dtype=jnp.int32))
        allowed = (tree_mask[request] > 0)[:, None, None, :]
        tree_scores = jnp.einsum('nkgd,jkd->nkgj', request_query, tree_keys[request]) / math.sqrt(HD)
        tree_scores = jnp.where(allowed, tree_scores, masked_score)
        overall = jnp.maximum(lax.optimization_barrier(jnp.max(maxima, axis=0)), lax.optimization_barrier(jnp.max(tree_scores, axis=-1)))
        rescale = jnp.exp(maxima - overall[None]) * sums
        numerator = lax.optimization_barrier(jnp.sum(rescale[..., None] * partial_out.astype(jnp.float32), axis=0))
        denominator = lax.optimization_barrier(jnp.sum(rescale, axis=0))
        tree_weights = jnp.where(allowed, jnp.exp(tree_scores - overall[..., None]), 0.0)
        numerator = numerator + jnp.einsum('nkgj,jkd->nkgd', rounded(tree_weights), tree_values[request])
        denominator = denominator + lax.optimization_barrier(jnp.sum(tree_weights, axis=-1))
        attended = (numerator / denominator[..., None]).astype(jnp.bfloat16)
        outputs.append(attended.reshape(NODES, HQ * HD))
    attended = jnp.concatenate(outputs, axis=0)
    projected = jnp.dot(attended, output_weight, preferred_element_type=jnp.float32)
    feature = (residual.astype(jnp.float32) + projected).astype(jnp.bfloat16)
    squares = lax.optimization_barrier(jnp.sum(jnp.square(feature.astype(jnp.float32)), axis=1))
    inverse = lax.rsqrt(squares / D + epsilon)
    normed = (feature.astype(jnp.float32) * inverse[:, None] * norm_gain.astype(jnp.float32)[None, :]).astype(jnp.bfloat16)
    row_ids = (jnp.arange(REQS, dtype=jnp.int32)[:, None] * NODES + parents).reshape(ROWS).astype(jnp.int32)
    chosen_rows = jnp.take(normed, row_ids, axis=0)
    draft_projection = jnp.dot(chosen_rows, draft_weight, preferred_element_type=jnp.float32).astype(jnp.bfloat16)
    return (feature, draft_projection)
```

```python
import functools
import math

import jax
import jax.numpy as jnp
from jax import lax
from jax.experimental import pallas as pl
from jax.experimental.pallas import tpu as pltpu
from jax.sharding import PartitionSpec as P

MESH = pl.DeviceIdType.MESH
masked_score = -1e30
epsilon = 1e-05


def attend(stacked, keys, values, live, scale):
    scores = lax.dot_general(
        stacked, keys, (((1,), (1,)), ((), ())), preferred_element_type=jnp.float32
    ) * scale
    scores = jnp.where(live, scores, masked_score)
    top = jnp.max(scores, axis=1, keepdims=True)
    weights = jnp.where(live, jnp.exp(scores - top), 0.0)
    total = jnp.sum(weights, axis=1, keepdims=True)
    mixed = jnp.dot(weights.astype(jnp.bfloat16), values, preferred_element_type=jnp.float32)
    return top, total, mixed / jnp.where(total > 0, total, 1.0)


def kernel(
    n,
    chunks,
    groups,
    q_ref,
    tree_ref,
    scales_ref,
    bits_ref,
    table_ref,
    lengths_ref,
    parents_ref,
    mask_ref,
    residual_ref,
    gain_ref,
    codes_hbm,
    weight_hbm,
    draft_hbm,
    feature_ref,
    drafted_ref,
    cache,
    weight,
    draft,
    q_all,
    t_send,
    t_all,
    b_send,
    b_recv,
    s_send,
    s_recv,
    t_out,
    t_stat,
    attended,
    c_send,
    c_recv,
    own,
    scaled,
    d_send,
    d_recv,
    d_own,
    sq_send,
    sq_recv,
    local_sem,
    weight_sem,
    draft_sem,
    q_sems,
    t_sems,
    b_sems,
    s_sems,
    c_sems,
    d_sems,
    sq_sems,
):
    me = lax.axis_index("tensor")
    rows, width = q_ref.shape
    slots, kv_heads, _, page, hd = cache.shape
    requests = lengths_ref.shape[0]
    nodes = rows // requests
    per = requests // chunks
    span = per * nodes
    heads = width // hd
    gh = min(groups, heads)
    kv_dev = heads // gh
    pages = table_ref.shape[1] // n
    block = pages * page
    tree_rows = tree_ref.shape[0]
    tree_width = kv_dev * hd
    out_width = draft.shape[2]
    scale = 1.0 / math.sqrt(hd)
    half = 128 // 2
    f32, bf16 = jnp.float32, jnp.bfloat16

    def ahead(k):
        return lax.rem(me + k, n)

    def behind(k):
        return lax.rem(me + n - k, n)

    def remote(src, dst, sems, index, k):
        return pltpu.make_async_remote_copy(
            src_ref=src,
            dst_ref=dst,
            send_sem=sems.at[(0, *index)],
            recv_sem=sems.at[(1, *index)],
            device_id={"tensor": ahead(k)},
            device_id_type=MESH,
        )

    def send_q(c, k):
        return remote(q_all.at[c, 0], q_all.at[c, k], q_sems, (c, k), k)

    def send_t(k):
        at = pl.ds(pl.multiple_of(me * tree_rows, tree_rows), tree_rows)
        return remote(t_send.at[k], t_all.at[:, at, :], t_sems, (k,), k)

    def send_b(c, k):
        return remote(b_send.at[c, n - k], b_recv.at[c, k], b_sems, (c, k), k)

    def send_s(c, k):
        return remote(s_send.at[c, n - k], s_recv.at[c, k], s_sems, (c, k), k)

    def send_c(c, k):
        return remote(c_send.at[c, k], c_recv.at[c, k], c_sems, (c, k), k)

    def send_d(c, k):
        return remote(d_send.at[c, k], d_recv.at[c, k], d_sems, (c, k), k)

    def send_sq(c, k):
        return remote(sq_send.at[c], sq_recv.at[c, k], sq_sems, (c, k), k)

    def load_weight(k):
        at = pl.ds(pl.multiple_of(ahead(k) * width, width), width)
        return pltpu.make_async_copy(weight_hbm.at[:, at], weight.at[k], weight_sem.at[k])

    def load_draft(k):
        at = pl.ds(pl.multiple_of(ahead(k) * out_width, out_width), out_width)
        return pltpu.make_async_copy(draft_hbm.at[:, at], draft.at[k], draft_sem.at[k])

    load_cache = pltpu.make_async_copy(codes_hbm, cache, local_sem)
    load_cache.start()

    barrier = pltpu.get_barrier_semaphore()
    for k in range(1, n):
        pl.semaphore_signal(
            barrier, inc=1, device_id={"tensor": ahead(k)}, device_id_type=MESH
        )
    for c in range(chunks):
        q_all[c, 0] = q_ref[c * span : (c + 1) * span, :]
    for k in range(n):
        first = ahead(k) * heads // groups
        for part in range(2):
            at = pl.ds(pl.multiple_of((part * kv_heads + first) * hd, hd), tree_width)
            t_send[k, part] = tree_ref[:, at].astype(t_send.dtype)
    mine = pl.ds(pl.multiple_of(me * tree_rows, tree_rows), tree_rows)
    t_all[:, mine, :] = t_send[0]
    pl.semaphore_wait(barrier, n - 1)

    for c in range(chunks):
        for k in range(1, n):
            send_q(c, k).start()
    for k in range(1, n):
        send_t(k).start()
    for k in range(n):
        load_weight(k).start()
    for k in range(n):
        load_draft(k).start()

    load_cache.wait()

    @pl.loop(0, slots)
    def _(slot):
        for g in range(kv_heads):
            level = jnp.full((1, hd), jnp.left_shift(jnp.int32(1), bits_ref[g]), jnp.int32)
            level = level.astype(f32)
            for part in range(2):
                ratio = scales_ref[slot, g, part : part + 1, :] / level
                codes = cache[slot, g, part].astype(f32)
                cache[slot, g, part] = (ratio * (2.0 * codes - level + 1.0)).astype(bf16)

    lane = lax.broadcasted_iota(jnp.int32, (nodes, 128), 1)
    place = lax.broadcasted_iota(jnp.int32, (1, block), 1) + me * block

    def stack(c, k, r, j):
        at = slice(r * nodes, (r + 1) * nodes)
        cols = [slice((j * gh + h) * hd, (j * gh + h + 1) * hd) for h in range(gh)]
        return jnp.concatenate([q_all[c, k, at, col] for col in cols], axis=0)

    def add_stats(stats, r, j, top, total):
        for h in range(gh):
            at = r * heads + j * gh + h
            part = slice(h * nodes, (h + 1) * nodes)
            stats = jnp.where(lane == at, top[part], stats)
            stats = jnp.where(lane == half + at, total[part], stats)
        return stats

    @pl.loop(0, chunks)
    def _(c):
        @pl.loop(0, n)
        def _(k):
            @pl.when(k > 0)
            def _():
                send_q(c, k).wait_recv()

            first = behind(k) * heads // groups
            stats = jnp.zeros((nodes, 128), f32)
            for r in range(per):
                request = c * per + r
                ids = [table_ref[request, me * pages + p] for p in range(pages)]
                live = place < lengths_ref[request]
                for j in range(kv_dev):
                    keys, values = (
                        jnp.concatenate([cache[i, first + j, part] for i in ids], axis=0)
                        for part in range(2)
                    )
                    top, total, mixed = attend(stack(c, k, r, j), keys, values, live, scale)
                    stats = add_stats(stats, r, j, top, total)
                    mixed = mixed.astype(bf16)
                    for h in range(gh):
                        b_send[
                            c,
                            k,
                            r * nodes : (r + 1) * nodes,
                            (j * gh + h) * hd : (j * gh + h + 1) * hd,
                        ] = mixed[h * nodes : (h + 1) * nodes]
            s_send[c, k] = stats

            @pl.when(k > 0)
            def _():
                send_b(c, n - k).start()
                send_s(c, n - k).start()

    for k in range(1, n):
        send_t(k).wait_recv()

    @pl.loop(0, chunks)
    def _(c):
        stats = jnp.zeros((nodes, 128), f32)
        for r in range(per):
            request = c * per + r
            allowed = jnp.concatenate([mask_ref[request]] * gh, axis=0) > 0
            at = pl.ds(pl.multiple_of(request * nodes, nodes), nodes)
            for j in range(kv_dev):
                col = slice(j * hd, (j + 1) * hd)
                keys, values = (t_all[part, at, col].astype(bf16) for part in range(2))
                top, total, mixed = attend(stack(c, 0, r, j), keys, values, allowed, scale)
                stats = add_stats(stats, r, j, top, total)
                for h in range(gh):
                    t_out[
                        c,
                        r * nodes : (r + 1) * nodes,
                        (j * gh + h) * hd : (j * gh + h + 1) * hd,
                    ] = mixed[h * nodes : (h + 1) * nodes]
        t_stat[c] = stats

    for k in range(n):
        load_weight(k).wait()

    tile = min(width, 512)

    @pl.loop(0, chunks)
    def _(c):
        for k in range(1, n):
            send_b(c, k).wait_recv()
            send_s(c, k).wait_recv()
        stats = [t_stat[c], s_send[c, 0]] + [s_recv[c, k] for k in range(1, n)]
        overall = functools.reduce(jnp.maximum, stats)
        shares = [jnp.exp(one - overall) * pltpu.roll(one, half, 1) for one in stats]
        inverse = 1.0 / functools.reduce(jnp.add, shares)
        shares = [one * inverse for one in shares]
        for r in range(per):
            at = slice(r * nodes, (r + 1) * nodes)
            for h in range(heads):
                col = slice(h * hd, (h + 1) * hd)
                i = r * heads + h
                blocks = [t_out[c, at, col], b_send[c, 0, at, col].astype(f32)]
                blocks += [b_recv[c, k, at, col].astype(f32) for k in range(1, n)]
                mixed = functools.reduce(
                    jnp.add, [one[:, i : i + 1] * b for one, b in zip(shares, blocks)]
                )
                attended[at, col] = mixed.astype(bf16)

        @pl.loop(1, n)
        def _(k):
            @pl.loop(0, width // tile)
            def _(j):
                cols = pl.ds(pl.multiple_of(j * tile, tile), tile)
                c_send[c, k, :, cols] = jnp.dot(
                    attended[...], weight[k, :, cols], preferred_element_type=f32
                ).astype(bf16)

            send_c(c, k).start()

        @pl.loop(0, width // tile)
        def _(j):
            cols = pl.ds(pl.multiple_of(j * tile, tile), tile)
            own[c, :, cols] = jnp.dot(
                attended[...], weight[0, :, cols], preferred_element_type=f32
            )

    for k in range(n):
        load_draft(k).wait()

    row_of = lax.broadcasted_iota(jnp.int32, (span, 128), 0)
    lane_of = lax.broadcasted_iota(jnp.int32, (span, 128), 1)
    diagonal = row_of == lane_of

    @pl.loop(0, chunks)
    def _(c):
        for k in range(1, n):
            send_c(c, k).wait_recv()
        at = pl.ds(pl.multiple_of(c * span, span), span)

        def finish(j, squares):
            cols = pl.ds(pl.multiple_of(j * 128, 128), 128)
            total = own[c, :, cols]
            for k in range(1, n):
                total = total + c_recv[c, k, :, cols].astype(f32)
            feature = (residual_ref[at, cols].astype(f32) + total).astype(bf16)
            feature_ref[at, cols] = feature
            feature = feature.astype(f32)
            scaled[:, cols] = (feature * gain_ref[:, cols].astype(f32)).astype(bf16)
            return squares + feature * feature

        squares = lax.fori_loop(0, width // 128, finish, jnp.zeros((span, 128), f32))
        column = jnp.sum(squares, axis=1, keepdims=True)
        line = jnp.sum(jnp.where(diagonal, column, 0.0), axis=0, keepdims=True)
        sq_send[c] = jnp.broadcast_to(line, (8, 128))
        for k in range(1, n):
            send_sq(c, k).start()

        @pl.loop(1, n)
        def _(k):
            d_send[c, k] = jnp.dot(
                scaled[...], draft[k], preferred_element_type=f32
            ).astype(bf16)
            send_d(c, k).start()

        d_own[c] = jnp.dot(scaled[...], draft[0], preferred_element_type=f32)

    @pl.loop(0, chunks)
    def _(c):
        for k in range(1, n):
            send_sq(c, k).wait_recv()
            send_d(c, k).wait_recv()
        total = d_own[c]
        line = sq_send[c, 0:1, :]
        for k in range(1, n):
            total = total + d_recv[c, k].astype(f32)
            line = line + sq_recv[c, k, 0:1, :]
        column = jnp.sum(jnp.where(diagonal, line, 0.0), axis=1, keepdims=True)
        inverse = lax.rsqrt(column / (width * n) + epsilon)
        drafted = (total * inverse).astype(bf16)
        source = lax.broadcasted_iota(jnp.int32, (nodes, nodes), 0)
        for r in range(per):
            request = c * per + r
            chosen = (source == parents_ref[pl.ds(request, 1), :]).astype(f32).astype(bf16)
            moved = lax.dot_general(
                chosen,
                drafted[r * nodes : (r + 1) * nodes],
                (((0,), (0,)), ((), ())),
                preferred_element_type=f32,
            )
            to = pl.ds(pl.multiple_of(request * nodes, nodes), nodes)
            drafted_ref[to, :] = moved.astype(bf16)

    for k in range(1, n):
        send_t(k).wait_send()
        for c in range(chunks):
            for send in (send_q, send_b, send_s, send_c, send_d, send_sq):
                send(c, k).wait_send()


def shards(
    n,
    query_heads,
    queries,
    tree_states,
    cache_codes,
    cache_scales,
    bit_widths,
    page_table,
    lengths,
    parents,
    tree_mask,
    output_weight,
    residual,
    norm_gain,
    draft_weight,
):
    rows, width = queries.shape
    slots, kv_heads, _, page, hd = cache_codes.shape
    requests = lengths.shape[0]
    nodes = rows // requests
    groups = query_heads // kv_heads
    heads = width // hd
    chunks = 2 if requests % 2 == 0 else 1
    while requests // chunks * heads > 64 or requests // chunks * nodes > 128:
        chunks *= 2
    span = rows // chunks
    kv_dev = max(1, heads // groups)
    tree_rows = tree_states.shape[0]
    wire = jnp.bfloat16 if tree_rows % 16 == 0 else jnp.float32
    out_width = draft_weight.shape[1] // n
    f32, bf16 = jnp.float32, jnp.bfloat16
    dma = pltpu.SemaphoreType.DMA
    vmem, smem, hbm = (
        pl.BlockSpec(memory_space=space) for space in (pltpu.VMEM, pltpu.SMEM, pl.ANY)
    )
    sems = dma((2, chunks, n))
    return pl.pallas_call(
        functools.partial(kernel, n, chunks, groups),
        out_shape=(
            jax.ShapeDtypeStruct((rows, width), bf16),
            jax.ShapeDtypeStruct((rows, out_width), bf16),
        ),
        in_specs=[vmem, vmem, vmem, smem, smem, smem, vmem, vmem, vmem, vmem, hbm, hbm, hbm],
        out_specs=(vmem, vmem),
        scratch_shapes=[
            pltpu.VMEM(cache_codes.shape, bf16),
            pltpu.VMEM((n, width, width), bf16),
            pltpu.VMEM((n, width, out_width), bf16),
            pltpu.VMEM((chunks, n, span, width), bf16),
            pltpu.VMEM((n, 2, tree_rows, kv_dev * hd), wire),
            pltpu.VMEM((2, rows, kv_dev * hd), wire),
            pltpu.VMEM((chunks, n, span, width), bf16),
            pltpu.VMEM((chunks, n, span, width), bf16),
            pltpu.VMEM((chunks, n, nodes, 128), f32),
            pltpu.VMEM((chunks, n, nodes, 128), f32),
            pltpu.VMEM((chunks, span, width), f32),
            pltpu.VMEM((chunks, nodes, 128), f32),
            pltpu.VMEM((span, width), bf16),
            pltpu.VMEM((chunks, n, span, width), bf16),
            pltpu.VMEM((chunks, n, span, width), bf16),
            pltpu.VMEM((chunks, span, width), f32),
            pltpu.VMEM((span, width), bf16),
            pltpu.VMEM((chunks, n, span, out_width), bf16),
            pltpu.VMEM((chunks, n, span, out_width), bf16),
            pltpu.VMEM((chunks, span, out_width), f32),
            pltpu.VMEM((chunks, 8, 128), f32),
            pltpu.VMEM((chunks, n, 8, 128), f32),
            dma,
            dma((n,)),
            dma((n,)),
            sems,
            dma((2, n)),
            sems,
            sems,
            sems,
            sems,
            sems,
        ],
        compiler_params=pltpu.CompilerParams(
            collective_id=0, has_side_effects=True, vmem_limit_bytes=63 * 1024 * 1024
        ),
    )(
        queries,
        tree_states,
        cache_scales,
        bit_widths,
        page_table,
        lengths,
        parents,
        tree_mask,
        residual,
        norm_gain.reshape(1, -1),
        cache_codes,
        output_weight,
        draft_weight,
    )


def solution(mesh):
    n = mesh.shape["tensor"]
    placed = (
        P("dp", "tensor"),
        P(("dp", "tensor"), None),
        P(("dp", "tensor"), None, None, None, None),
        P(("dp", "tensor"), None, None, None),
        P("dp"),
        P("dp", None),
        P("dp"),
        P("dp", None),
        P("dp", None, None),
        P("tensor", None),
        P("dp", "tensor"),
        P("tensor"),
        P("tensor", None),
    )

    def run(*arrays):
        query_heads = arrays[0].shape[1] // arrays[2].shape[-1]
        return jax.shard_map(
            functools.partial(shards, n, query_heads),
            mesh=mesh,
            in_specs=placed,
            out_specs=(P("dp", "tensor"), P("dp", "tensor")),
            check_vma=False,
        )(*arrays)

    return run
```

```python
import functools
import math

import jax
import jax.numpy as jnp
from jax import lax
from jax.experimental import pallas as pl
from jax.experimental.pallas import tpu as pltpu
from jax.sharding import PartitionSpec as P

MESH = pl.DeviceIdType.MESH
masked_score = -1e30
epsilon = 1e-05


def attend(stacked, keys, values, live, scale):
    scores = lax.dot_general(
        stacked, keys, (((1,), (1,)), ((), ())), preferred_element_type=jnp.float32
    ) * scale
    scores = jnp.where(live, scores, masked_score)
    top = jnp.max(scores, axis=1, keepdims=True)
    weights = jnp.where(live, jnp.exp(scores - top), 0.0)
    total = jnp.sum(weights, axis=1, keepdims=True)
    mixed = jnp.dot(weights.astype(jnp.bfloat16), values, preferred_element_type=jnp.float32)
    return top, total, mixed / jnp.where(total > 0, total, 1.0)


def kernel(
    n,
    chunks,
    groups,
    q_ref,
    tree_ref,
    scales_ref,
    bits_ref,
    table_ref,
    lengths_ref,
    parents_ref,
    mask_ref,
    residual_ref,
    gain_ref,
    codes_hbm,
    weight_hbm,
    draft_hbm,
    feature_ref,
    drafted_ref,
    cache,
    weight,
    draft,
    q_all,
    t_send,
    t_all,
    b_send,
    b_recv,
    s_send,
    s_recv,
    t_out,
    t_stat,
    attended,
    c_send,
    c_recv,
    own,
    scaled,
    d_send,
    d_recv,
    d_own,
    sq_send,
    sq_recv,
    gain,
    local_sem,
    weight_sem,
    draft_sem,
    q_sems,
    t_sems,
    b_sems,
    s_sems,
    c_sems,
    d_sems,
    sq_sems,
):
    me = lax.axis_index("tensor")
    rows, width = q_ref.shape
    slots, kv_heads, _, page, hd = cache.shape
    requests = lengths_ref.shape[0]
    nodes = rows // requests
    per = requests // chunks
    span = per * nodes
    heads = width // hd
    gh = min(groups, heads)
    kv_dev = heads // gh
    pages = table_ref.shape[1] // n
    block = pages * page
    tree_rows = tree_ref.shape[0]
    tree_width = kv_dev * hd
    out_width = draft.shape[2]
    scale = 1.0 / math.sqrt(hd)
    half = 128 // 2
    f32, bf16 = jnp.float32, jnp.bfloat16

    relay = n == 4
    part_rows = span // 2

    def flipped(k):
        low = lax.rem(me + k, 2)
        return 2 * lax.rem(me // 2 + k // 2, 2) + low

    def ahead(k):
        return flipped(k) if relay else lax.rem(me + k, n)

    def behind(k):
        return flipped(k) if relay else lax.rem(me + n - k, n)

    def back(k):
        return k if relay else n - k

    def remote(src, dst, sems, index, k):
        return pltpu.make_async_remote_copy(
            src_ref=src,
            dst_ref=dst,
            send_sem=sems.at[(0, *index)],
            recv_sem=sems.at[(1, *index)],
            device_id={"tensor": ahead(k)},
            device_id_type=MESH,
        )

    def send_q(c, k):
        return remote(q_all.at[c, 0], q_all.at[c, k], q_sems, (c, k), k)

    def forward_q(c, i):
        rows_at = pl.ds(i * part_rows, part_rows)
        return remote(
            q_all.at[c, 1 + i, rows_at],
            q_all.at[c, 3, rows_at],
            q_sems,
            (c, 3 - 3 * i),
            2 - i,
        )

    def pass_c(c, i):
        rows_at = pl.ds(i * part_rows, part_rows)
        return remote(
            c_send.at[c, 3, rows_at], c_recv.at[c, 3, rows_at], c_sems, (c, 3 - 3 * i), 1 + i
        )

    def send_t(k):
        at = pl.ds(pl.multiple_of(me * tree_rows, tree_rows), tree_rows)
        return remote(t_send.at[k], t_all.at[:, at, :], t_sems, (k,), k)

    def send_b(c, k):
        return remote(b_send.at[c, back(k)], b_recv.at[c, k], b_sems, (c, k), k)

    def send_s(c, k):
        return remote(s_send.at[c, back(k)], s_recv.at[c, k], s_sems, (c, k), k)

    def send_c(c, k):
        return remote(c_send.at[c, k], c_recv.at[c, k], c_sems, (c, k), k)

    def send_d(c, k):
        return remote(d_send.at[c, k], d_recv.at[c, k], d_sems, (c, k), k)

    def send_sq(c, k):
        return remote(sq_send.at[c], sq_recv.at[c, k], sq_sems, (c, k), k)

    def load_weight(k):
        at = pl.ds(pl.multiple_of(ahead(k) * width, width), width)
        return pltpu.make_async_copy(weight_hbm.at[:, at], weight.at[k], weight_sem.at[k])

    def load_draft(k):
        at = pl.ds(pl.multiple_of(ahead(k) * out_width, out_width), out_width)
        return pltpu.make_async_copy(draft_hbm.at[:, at], draft.at[k], draft_sem.at[k])

    load_cache = pltpu.make_async_copy(codes_hbm, cache, local_sem)
    load_cache.start()
    gain[...] = gain_ref[...].astype(f32)

    barrier = pltpu.get_barrier_semaphore()
    for k in range(1, n):
        pl.semaphore_signal(
            barrier, inc=1, device_id={"tensor": ahead(k)}, device_id_type=MESH
        )
    for c in range(chunks):
        q_all[c, 0] = q_ref[c * span : (c + 1) * span, :]
    for k in range(n):
        first = ahead(k) * heads // groups
        for part in range(2):
            at = pl.ds(pl.multiple_of((part * kv_heads + first) * hd, hd), tree_width)
            t_send[k, part] = tree_ref[:, at].astype(t_send.dtype)
    mine = pl.ds(pl.multiple_of(me * tree_rows, tree_rows), tree_rows)
    t_all[:, mine, :] = t_send[0]
    pl.semaphore_wait(barrier, n - 1)

    near = range(1, 3 if relay else n)
    for c in range(chunks):
        for k in near:
            send_q(c, k).start()
    for k in range(1, n):
        send_t(k).start()
    for k in range(n):
        load_weight(k).start()
    for k in range(n):
        load_draft(k).start()

    load_cache.wait()

    @pl.loop(0, slots)
    def _(slot):
        for g in range(kv_heads):
            level = jnp.full((1, hd), jnp.left_shift(jnp.int32(1), bits_ref[g]), jnp.int32)
            level = level.astype(f32)
            for part in range(2):
                ratio = scales_ref[slot, g, part : part + 1, :] / level
                codes = cache[slot, g, part].astype(f32)
                cache[slot, g, part] = (ratio * (2.0 * codes - level + 1.0)).astype(bf16)

    lane = lax.broadcasted_iota(jnp.int32, (nodes, 128), 1)
    place = lax.broadcasted_iota(jnp.int32, (1, block), 1) + me * block

    def stack(c, k, r, j):
        at = slice(r * nodes, (r + 1) * nodes)
        cols = [slice((j * gh + h) * hd, (j * gh + h + 1) * hd) for h in range(gh)]
        return jnp.concatenate([q_all[c, k, at, col] for col in cols], axis=0)

    def add_stats(stats, r, j, top, total):
        for h in range(gh):
            at = r * heads + j * gh + h
            part = slice(h * nodes, (h + 1) * nodes)
            stats = jnp.where(lane == at, top[part], stats)
            stats = jnp.where(lane == half + at, total[part], stats)
        return stats

    def receive_q(c):
        for k in (1, 2):
            send_q(c, k).wait_recv()
        for i in range(2):
            forward_q(c, i).start()

    @pl.loop(0, chunks * n)
    def _(step):
        later = jnp.maximum(step - chunks, 0)
        own_step = step < chunks
        c = jnp.where(own_step, step, later // (n - 1))
        k = jnp.where(own_step, 0, 1 + lax.rem(later, n - 1))

        if n > 0:
            if relay:
                @pl.when(step == chunks)
                def _():
                    receive_q(0)

                @pl.when(k == 3)
                def _():
                    @pl.when(c < chunks - 1)
                    def _():
                        receive_q(c + 1)

                    for i in range(2):
                        forward_q(c, i).wait_recv()
            else:
                @pl.when(k > 0)
                def _():
                    send_q(c, k).wait_recv()

            first = behind(k) * heads // groups
            stats = jnp.zeros((nodes, 128), f32)
            for r in range(per):
                request = c * per + r
                ids = [table_ref[request, me * pages + p] for p in range(pages)]
                live = place < lengths_ref[request]
                for j in range(kv_dev):
                    keys, values = (
                        jnp.concatenate([cache[i, first + j, part] for i in ids], axis=0)
                        for part in range(2)
                    )
                    top, total, mixed = attend(stack(c, k, r, j), keys, values, live, scale)
                    stats = add_stats(stats, r, j, top, total)
                    mixed = mixed.astype(bf16)
                    for h in range(gh):
                        b_send[
                            c,
                            k,
                            r * nodes : (r + 1) * nodes,
                            (j * gh + h) * hd : (j * gh + h + 1) * hd,
                        ] = mixed[h * nodes : (h + 1) * nodes]
            s_send[c, k] = stats

            @pl.when(k > 0)
            def _():
                send_b(c, back(k)).start()
                send_s(c, back(k)).start()

    for k in range(1, n):
        send_t(k).wait_recv()

    @pl.loop(0, chunks)
    def _(c):
        stats = jnp.zeros((nodes, 128), f32)
        for r in range(per):
            request = c * per + r
            allowed = jnp.concatenate([mask_ref[request]] * gh, axis=0) > 0
            at = pl.ds(pl.multiple_of(request * nodes, nodes), nodes)
            for j in range(kv_dev):
                col = slice(j * hd, (j + 1) * hd)
                keys, values = (t_all[part, at, col].astype(bf16) for part in range(2))
                top, total, mixed = attend(stack(c, 0, r, j), keys, values, allowed, scale)
                stats = add_stats(stats, r, j, top, total)
                for h in range(gh):
                    t_out[
                        c,
                        r * nodes : (r + 1) * nodes,
                        (j * gh + h) * hd : (j * gh + h + 1) * hd,
                    ] = mixed[h * nodes : (h + 1) * nodes]
        t_stat[c] = stats

    for k in range(n):
        load_weight(k).wait()

    tile = min(width, 512)

    @pl.loop(0, chunks)
    def _(c):
        for k in range(1, n):
            send_b(c, k).wait_recv()
            send_s(c, k).wait_recv()
        stats = [t_stat[c], s_send[c, 0]] + [s_recv[c, k] for k in range(1, n)]
        overall = functools.reduce(jnp.maximum, stats)
        shares = [jnp.exp(one - overall) * pltpu.roll(one, half, 1) for one in stats]
        inverse = 1.0 / functools.reduce(jnp.add, shares)
        shares = [one * inverse for one in shares]
        for r in range(per):
            at = slice(r * nodes, (r + 1) * nodes)
            for h in range(heads):
                col = slice(h * hd, (h + 1) * hd)
                i = r * heads + h
                blocks = [t_out[c, at, col], b_send[c, 0, at, col].astype(f32)]
                blocks += [b_recv[c, k, at, col].astype(f32) for k in range(1, n)]
                mixed = functools.reduce(
                    jnp.add, [one[:, i : i + 1] * b for one, b in zip(shares, blocks)]
                )
                attended[at, col] = mixed.astype(bf16)

        def project(k, store):
            @pl.loop(0, width // tile)
            def _(j):
                cols = pl.ds(pl.multiple_of(j * tile, tile), tile)
                store(
                    cols,
                    jnp.dot(attended[...], weight[k, :, cols], preferred_element_type=f32),
                )

        def store_own(cols, product):
            own[c, :, cols] = product

        def store_send(k, cols, product):
            c_send[c, k, :, cols] = product.astype(bf16)

        def store_joined(k, cols, product):
            i = 2 - k
            lower = slice(i * part_rows, (i + 1) * part_rows)
            upper = slice((1 - i) * part_rows, (2 - i) * part_rows)
            passed = c_recv[c, 3, lower, cols].astype(f32)
            c_send[c, k, lower, cols] = (product[lower] + passed).astype(bf16)
            c_send[c, k, upper, cols] = product[upper].astype(bf16)

        if relay:
            project(3, functools.partial(store_send, 3))
            for i in range(2):
                pass_c(c, i).start()
            project(0, store_own)
            for k in (1, 2):
                pass_c(c, 2 - k).wait_recv()
                project(k, functools.partial(store_joined, k))
                send_c(c, k).start()
        else:
            @pl.loop(1, n)
            def _(k):
                project(k, functools.partial(store_send, k))
                send_c(c, k).start()

            project(0, store_own)

    for k in range(n):
        load_draft(k).wait()

    row_of = lax.broadcasted_iota(jnp.int32, (span, 128), 0)
    lane_of = lax.broadcasted_iota(jnp.int32, (span, 128), 1)
    diagonal = row_of == lane_of

    @pl.loop(0, chunks)
    def _(c):
        for k in near:
            send_c(c, k).wait_recv()
        at = pl.ds(pl.multiple_of(c * span, span), span)

        def finish(j, squares):
            cols = pl.ds(pl.multiple_of(j * 128, 128), 128)
            total = own[c, :, cols]
            for k in near:
                total = total + c_recv[c, k, :, cols].astype(f32)
            feature = (residual_ref[at, cols].astype(f32) + total).astype(bf16)
            feature_ref[at, cols] = feature
            feature = feature.astype(f32)
            scaled[:, cols] = (feature * gain[pl.ds(j, 1), :]).astype(bf16)
            return squares + feature * feature

        squares = lax.fori_loop(0, width // 128, finish, jnp.zeros((span, 128), f32))
        column = jnp.sum(squares, axis=1, keepdims=True)
        line = jnp.sum(jnp.where(diagonal, column, 0.0), axis=0, keepdims=True)
        sq_send[c] = jnp.broadcast_to(line, (8, 128))
        for k in range(1, n):
            send_sq(c, k).start()

        @pl.loop(1, n)
        def _(k):
            d_send[c, k] = jnp.dot(
                scaled[...], draft[k], preferred_element_type=f32
            ).astype(bf16)
            send_d(c, k).start()

        d_own[c] = jnp.dot(scaled[...], draft[0], preferred_element_type=f32)

    @pl.loop(0, chunks)
    def _(c):
        for k in range(1, n):
            send_sq(c, k).wait_recv()
            send_d(c, k).wait_recv()
        total = d_own[c]
        line = sq_send[c, 0:1, :]
        for k in range(1, n):
            total = total + d_recv[c, k].astype(f32)
            line = line + sq_recv[c, k, 0:1, :]
        column = jnp.sum(jnp.where(diagonal, line, 0.0), axis=1, keepdims=True)
        inverse = lax.rsqrt(column / (width * n) + epsilon)
        drafted = (total * inverse).astype(bf16)
        source = lax.broadcasted_iota(jnp.int32, (nodes, nodes), 0)
        for r in range(per):
            request = c * per + r
            chosen = (source == parents_ref[pl.ds(request, 1), :]).astype(f32).astype(bf16)
            moved = lax.dot_general(
                chosen,
                drafted[r * nodes : (r + 1) * nodes],
                (((0,), (0,)), ((), ())),
                preferred_element_type=f32,
            )
            to = pl.ds(pl.multiple_of(request * nodes, nodes), nodes)
            drafted_ref[to, :] = moved.astype(bf16)

    for k in range(1, n):
        send_t(k).wait_send()
        for c in range(chunks):
            for send in (send_b, send_s, send_d, send_sq):
                send(c, k).wait_send()
    for c in range(chunks):
        for k in near:
            send_q(c, k).wait_send()
            send_c(c, k).wait_send()
        if relay:
            for i in range(2):
                forward_q(c, i).wait_send()
                pass_c(c, i).wait_send()


def hand_over(feature_ref, drafted_ref, feature_out, drafted_out, sems):
    pairs = ((feature_ref, feature_out), (drafted_ref, drafted_out))
    copies = [
        pltpu.make_async_copy(source, target, sems.at[i])
        for i, (source, target) in enumerate(pairs)
    ]
    for copy in copies:
        copy.start()
    for copy in copies:
        copy.wait()


def shards(
    n,
    query_heads,
    queries,
    tree_states,
    cache_codes,
    cache_scales,
    bit_widths,
    page_table,
    lengths,
    parents,
    tree_mask,
    output_weight,
    residual,
    norm_gain,
    draft_weight,
):
    rows, width = queries.shape
    slots, kv_heads, _, page, hd = cache_codes.shape
    requests = lengths.shape[0]
    nodes = rows // requests
    groups = query_heads // kv_heads
    heads = width // hd
    chunks = 2 if requests % 2 == 0 else 1
    while requests // chunks * heads > 64 or requests // chunks * nodes > 128:
        chunks *= 2
    span = rows // chunks
    kv_dev = max(1, heads // groups)
    tree_rows = tree_states.shape[0]
    wire = jnp.bfloat16 if tree_rows % 16 == 0 else jnp.float32
    out_width = draft_weight.shape[1] // n
    f32, bf16 = jnp.float32, jnp.bfloat16
    dma = pltpu.SemaphoreType.DMA
    vmem, smem, hbm = (
        pl.BlockSpec(memory_space=space) for space in (pltpu.VMEM, pltpu.SMEM, pl.ANY)
    )
    sems = dma((2, chunks, n))
    results = pl.pallas_call(
        functools.partial(kernel, n, chunks, groups),
        out_shape=(
            jax.ShapeDtypeStruct((rows, width), bf16),
            jax.ShapeDtypeStruct((rows, out_width), bf16),
        ),
        in_specs=[vmem, vmem, vmem, smem, smem, smem, vmem, vmem, vmem, vmem, hbm, hbm, hbm],
        out_specs=(vmem, vmem),
        scratch_shapes=[
            pltpu.VMEM(cache_codes.shape, bf16),
            pltpu.VMEM((n, width, width), bf16),
            pltpu.VMEM((n, width, out_width), bf16),
            pltpu.VMEM((chunks, n, span, width), bf16),
            pltpu.VMEM((n, 2, tree_rows, kv_dev * hd), wire),
            pltpu.VMEM((2, rows, kv_dev * hd), wire),
            pltpu.VMEM((chunks, n, span, width), bf16),
            pltpu.VMEM((chunks, n, span, width), bf16),
            pltpu.VMEM((chunks, n, nodes, 128), f32),
            pltpu.VMEM((chunks, n, nodes, 128), f32),
            pltpu.VMEM((chunks, span, width), f32),
            pltpu.VMEM((chunks, nodes, 128), f32),
            pltpu.VMEM((span, width), bf16),
            pltpu.VMEM((chunks, n, span, width), bf16),
            pltpu.VMEM((chunks, n, span, width), bf16),
            pltpu.VMEM((chunks, span, width), f32),
            pltpu.VMEM((span, width), bf16),
            pltpu.VMEM((chunks, n, span, out_width), bf16),
            pltpu.VMEM((chunks, n, span, out_width), bf16),
            pltpu.VMEM((chunks, span, out_width), f32),
            pltpu.VMEM((chunks, 8, 128), f32),
            pltpu.VMEM((chunks, n, 8, 128), f32),
            pltpu.VMEM((width // 128, 128), f32),
            dma,
            dma((n,)),
            dma((n,)),
            sems,
            dma((2, n)),
            sems,
            sems,
            sems,
            sems,
            sems,
        ],
        compiler_params=pltpu.CompilerParams(
            collective_id=0, has_side_effects=True, vmem_limit_bytes=63 * 1024 * 1024
        ),
    )(
        queries,
        tree_states,
        cache_scales,
        bit_widths,
        page_table,
        lengths,
        parents,
        tree_mask,
        residual,
        norm_gain.reshape(-1, 128),
        cache_codes,
        output_weight,
        draft_weight,
    )
    return pl.pallas_call(
        hand_over,
        out_shape=tuple(jax.ShapeDtypeStruct(one.shape, one.dtype) for one in results),
        in_specs=[hbm, hbm],
        out_specs=(hbm, hbm),
        scratch_shapes=[dma((2,))],
        compiler_params=pltpu.CompilerParams(vmem_limit_bytes=63 * 1024 * 1024),
    )(*results)


def solution(mesh):
    n = mesh.shape["tensor"]
    placed = (
        P("dp", "tensor"),
        P(("dp", "tensor"), None),
        P(("dp", "tensor"), None, None, None, None),
        P(("dp", "tensor"), None, None, None),
        P("dp"),
        P("dp", None),
        P("dp"),
        P("dp", None),
        P("dp", None, None),
        P("tensor", None),
        P("dp", "tensor"),
        P("tensor"),
        P("tensor", None),
    )

    def run(*arrays):
        query_heads = arrays[0].shape[1] // arrays[2].shape[-1]
        return jax.shard_map(
            functools.partial(shards, n, query_heads),
            mesh=mesh,
            in_specs=placed,
            out_specs=(P("dp", "tensor"), P("dp", "tensor")),
            check_vma=False,
        )(*arrays)

    return run
```

```python
import functools
import math

import jax
import jax.numpy as jnp
from jax import lax
from jax.experimental import pallas as pl
from jax.experimental.pallas import tpu as pltpu
from jax.sharding import PartitionSpec as P

MESH = pl.DeviceIdType.MESH
masked_score = -1e30
epsilon = 1e-05


def attend(stacked, keys, values, live, scale):
    floor = masked_score / scale
    raw = lax.dot_general(
        keys, stacked, (((1,), (1,)), ((), ())), preferred_element_type=jnp.float32
    )
    raw = jnp.where(live, raw, floor)
    top = jnp.max(raw, axis=0, keepdims=True)
    base = jnp.where(top == floor, 0.0, top)
    weights = jnp.exp2((raw - base) * (scale * math.log2(math.e)))
    total = jnp.sum(weights, axis=0, keepdims=True)
    mixed = lax.dot_general(
        values,
        weights.astype(jnp.bfloat16),
        (((0,), (0,)), ((), ())),
        preferred_element_type=jnp.float32,
    )
    return top * scale, total, mixed * (1.0 / jnp.where(total > 0, total, 1.0))


def kernel(
    n,
    chunks,
    groups,
    q_ref,
    tree_ref,
    scales_ref,
    bits_ref,
    table_ref,
    lengths_ref,
    parents_ref,
    mask_ref,
    residual_ref,
    gain_ref,
    codes_hbm,
    weight_hbm,
    draft_hbm,
    feature_ref,
    drafted_ref,
    cache,
    weight,
    draft,
    q_all,
    t_send,
    t_all,
    b_send,
    b_recv,
    s_send,
    s_recv,
    t_out,
    t_stat,
    attended,
    c_send,
    c_recv,
    own,
    scaled,
    d_send,
    d_recv,
    d_own,
    sq_send,
    sq_recv,
    gain,
    local_sem,
    weight_sem,
    draft_sem,
    q_sems,
    t_sems,
    b_sems,
    s_sems,
    c_sems,
    d_sems,
    sq_sems,
):
    me = lax.axis_index("tensor")
    rows, width = q_ref.shape
    slots, kv_heads, _, page, hd = cache.shape
    requests = lengths_ref.shape[0]
    nodes = rows // requests
    per = requests // chunks
    span = per * nodes
    heads = width // hd
    gh = min(groups, heads)
    kv_dev = heads // gh
    pages = table_ref.shape[1] // n
    block = pages * page
    tree_rows = tree_ref.shape[0]
    tree_width = kv_dev * hd
    out_width = draft.shape[2]
    scale = 1.0 / math.sqrt(hd)
    lanes = gh * nodes
    f32, bf16 = jnp.float32, jnp.bfloat16

    relay = n == 4
    part_rows = span // 2

    def flipped(k):
        low = lax.rem(me + k, 2)
        return 2 * lax.rem(me // 2 + k // 2, 2) + low

    def ahead(k):
        return flipped(k) if relay else lax.rem(me + k, n)

    def behind(k):
        return flipped(k) if relay else lax.rem(me + n - k, n)

    def back(k):
        return k if relay else n - k

    def remote(src, dst, sems, index, k):
        return pltpu.make_async_remote_copy(
            src_ref=src,
            dst_ref=dst,
            send_sem=sems.at[(0, *index)],
            recv_sem=sems.at[(1, *index)],
            device_id={"tensor": ahead(k)},
            device_id_type=MESH,
        )

    def send_q(c, k):
        return remote(q_all.at[c, 0], q_all.at[c, k], q_sems, (c, k), k)

    def forward_q(c, i):
        rows_at = pl.ds(i * part_rows, part_rows)
        return remote(
            q_all.at[c, 1 + i, rows_at],
            q_all.at[c, 3, rows_at],
            q_sems,
            (c, 3 - 3 * i),
            2 - i,
        )

    def pass_c(c, i):
        rows_at = pl.ds(i * part_rows, part_rows)
        return remote(
            c_send.at[c, 3, rows_at], c_recv.at[c, 3, rows_at], c_sems, (c, 3 - 3 * i), 1 + i
        )

    def send_t(k):
        at = pl.ds(pl.multiple_of(me * tree_rows, tree_rows), tree_rows)
        return remote(t_send.at[k], t_all.at[:, at, :], t_sems, (k,), k)

    def send_b(c, k):
        return remote(b_send.at[c, back(k)], b_recv.at[c, k], b_sems, (c, k), k)

    def send_s(c, k):
        return remote(s_send.at[c, back(k)], s_recv.at[c, k], s_sems, (c, k), k)

    def send_c(c, k):
        return remote(c_send.at[c, k], c_recv.at[c, k], c_sems, (c, k), k)

    def send_d(c, k):
        return remote(d_send.at[c, k], d_recv.at[c, k], d_sems, (c, k), k)

    def send_sq(c, k):
        return remote(sq_send.at[c], sq_recv.at[c, k], sq_sems, (c, k), k)

    def load_weight(k):
        at = pl.ds(pl.multiple_of(ahead(k) * width, width), width)
        return pltpu.make_async_copy(weight_hbm.at[:, at], weight.at[k], weight_sem.at[k])

    def load_draft(k):
        at = pl.ds(pl.multiple_of(ahead(k) * out_width, out_width), out_width)
        return pltpu.make_async_copy(draft_hbm.at[:, at], draft.at[k], draft_sem.at[k])

    load_cache = pltpu.make_async_copy(codes_hbm, cache, local_sem)
    load_cache.start()
    gain[...] = gain_ref[...].astype(f32)

    barrier = pltpu.get_barrier_semaphore()
    for k in range(1, n):
        pl.semaphore_signal(
            barrier, inc=1, device_id={"tensor": ahead(k)}, device_id_type=MESH
        )
    for c in range(chunks):
        q_all[c, 0] = q_ref[c * span : (c + 1) * span, :]
    for k in range(n):
        first = ahead(k) * heads // groups
        for part in range(2):
            at = pl.ds(pl.multiple_of((part * kv_heads + first) * hd, hd), tree_width)
            t_send[k, part] = tree_ref[:, at].astype(t_send.dtype)
    mine = pl.ds(pl.multiple_of(me * tree_rows, tree_rows), tree_rows)
    t_all[:, mine, :] = t_send[0]
    pl.semaphore_wait(barrier, n - 1)

    near = range(1, 3 if relay else n)
    for c in range(chunks):
        for k in near:
            send_q(c, k).start()
    for k in range(1, n):
        send_t(k).start()
    for k in range(n):
        load_weight(k).start()
    for k in range(n):
        load_draft(k).start()

    load_cache.wait()

    @pl.loop(0, slots)
    def _(slot):
        for g in range(kv_heads):
            level = jnp.full((1, hd), jnp.left_shift(jnp.int32(1), bits_ref[g]), jnp.int32)
            level = level.astype(f32)
            for part in range(2):
                ratio = scales_ref[slot, g, part : part + 1, :] / level
                codes = cache[slot, g, part].astype(f32)
                cache[slot, g, part] = (ratio * (2.0 * codes - level + 1.0)).astype(bf16)

    place = lax.broadcasted_iota(jnp.int32, (block, lanes), 0)

    def stack(c, k, r, j):
        at = slice(r * nodes, (r + 1) * nodes)
        cols = [slice((j * gh + h) * hd, (j * gh + h + 1) * hd) for h in range(gh)]
        return jnp.concatenate([q_all[c, k, at, col] for col in cols], axis=0)

    def receive_q(c):
        for k in (1, 2):
            send_q(c, k).wait_recv()
        for i in range(2):
            forward_q(c, i).start()

    @pl.loop(0, chunks * n)
    def _(step):
        later = jnp.maximum(step - chunks, 0)
        own_step = step < chunks
        c = jnp.where(own_step, step, later // (n - 1))
        k = jnp.where(own_step, 0, 1 + lax.rem(later, n - 1))

        if n > 0:
            if relay:
                @pl.when(step == chunks)
                def _():
                    receive_q(0)

                @pl.when(k == 3)
                def _():
                    @pl.when(c < chunks - 1)
                    def _():
                        receive_q(c + 1)

                    for i in range(2):
                        forward_q(c, i).wait_recv()
            else:
                @pl.when(k > 0)
                def _():
                    send_q(c, k).wait_recv()

            first = behind(k) * heads // groups
            for r in range(per):
                request = c * per + r
                ids = [table_ref[request, me * pages + p] for p in range(pages)]
                live = place < lengths_ref[request] - me * block
                for j in range(kv_dev):
                    u = r * kv_dev + j
                    keys, values = (
                        jnp.concatenate([cache[i, first + j, part] for i in ids], axis=0)
                        for part in range(2)
                    )
                    top, total, mixed = attend(stack(c, k, r, j), keys, values, live, scale)
                    s_send[c, k, 2 * u : 2 * u + 1, :] = top
                    s_send[c, k, 2 * u + 1 : 2 * u + 2, :] = total
                    b_send[c, k, u] = mixed.astype(bf16)

            @pl.when(k > 0)
            def _():
                send_b(c, back(k)).start()
                send_s(c, back(k)).start()

    for k in range(1, n):
        send_t(k).wait_recv()

    turn_row = lax.broadcasted_iota(jnp.int32, (nodes, lanes), 0)
    turn_lane = lax.broadcasted_iota(jnp.int32, (nodes, lanes), 1)
    turn = (turn_row == lax.rem(turn_lane, nodes)).astype(f32).astype(bf16)

    @pl.loop(0, chunks)
    def _(c):
        for r in range(per):
            request = c * per + r
            turned = lax.dot_general(
                mask_ref[request].astype(f32).astype(bf16),
                turn,
                (((0,), (0,)), ((), ())),
                preferred_element_type=f32,
            )
            at = pl.ds(pl.multiple_of(request * nodes, nodes), nodes)
            for j in range(kv_dev):
                u = r * kv_dev + j
                col = slice(j * hd, (j + 1) * hd)
                keys, values = (t_all[part, at, col].astype(bf16) for part in range(2))
                top, total, mixed = attend(stack(c, 0, r, j), keys, values, turned > 0.5, scale)
                t_stat[c, 2 * u : 2 * u + 1, :] = top
                t_stat[c, 2 * u + 1 : 2 * u + 2, :] = total
                t_out[c, u] = mixed

    for k in range(n):
        load_weight(k).wait()

    tile = min(width, 512)

    @pl.loop(0, chunks)
    def _(c):
        for k in range(1, n):
            send_b(c, k).wait_recv()
            send_s(c, k).wait_recv()
        for u in range(per * kv_dev):
            tops, totals = (
                [t_stat[c, row], s_send[c, 0, row]] + [s_recv[c, k, row] for k in range(1, n)]
                for row in (slice(2 * u, 2 * u + 1), slice(2 * u + 1, 2 * u + 2))
            )
            overall = functools.reduce(jnp.maximum, tops)
            shares = [jnp.exp(one - overall) * total for one, total in zip(tops, totals)]
            inverse = 1.0 / functools.reduce(jnp.add, shares)
            blocks = [t_out[c, u], b_send[c, 0, u].astype(f32)]
            blocks += [b_recv[c, k, u].astype(f32) for k in range(1, n)]
            mixed = functools.reduce(
                jnp.add, [one * inverse * b for one, b in zip(shares, blocks)]
            )
            mixed = mixed.T.astype(bf16)
            r, j = u // kv_dev, u % kv_dev
            for h in range(gh):
                attended[
                    r * nodes : (r + 1) * nodes,
                    (j * gh + h) * hd : (j * gh + h + 1) * hd,
                ] = mixed[h * nodes : (h + 1) * nodes]

        def project(k, store):
            @pl.loop(0, width // tile)
            def _(j):
                cols = pl.ds(pl.multiple_of(j * tile, tile), tile)
                store(
                    cols,
                    jnp.dot(attended[...], weight[k, :, cols], preferred_element_type=f32),
                )

        def store_own(cols, product):
            own[c, :, cols] = product

        def store_send(k, cols, product):
            c_send[c, k, :, cols] = product.astype(bf16)

        def store_joined(k, cols, product):
            i = 2 - k
            lower = slice(i * part_rows, (i + 1) * part_rows)
            upper = slice((1 - i) * part_rows, (2 - i) * part_rows)
            passed = c_recv[c, 3, lower, cols].astype(f32)
            c_send[c, k, lower, cols] = (product[lower] + passed).astype(bf16)
            c_send[c, k, upper, cols] = product[upper].astype(bf16)

        if relay:
            project(3, functools.partial(store_send, 3))
            for i in range(2):
                pass_c(c, i).start()
            project(0, store_own)
            for k in (1, 2):
                pass_c(c, 2 - k).wait_recv()
                project(k, functools.partial(store_joined, k))
                send_c(c, k).start()
        else:
            @pl.loop(1, n)
            def _(k):
                project(k, functools.partial(store_send, k))
                send_c(c, k).start()

            project(0, store_own)

    for k in range(n):
        load_draft(k).wait()

    row_of = lax.broadcasted_iota(jnp.int32, (span, 128), 0)
    lane_of = lax.broadcasted_iota(jnp.int32, (span, 128), 1)
    diagonal = row_of == lane_of

    @pl.loop(0, chunks)
    def _(c):
        for k in near:
            send_c(c, k).wait_recv()
        at = pl.ds(pl.multiple_of(c * span, span), span)

        def finish(j, squares):
            cols = pl.ds(pl.multiple_of(j * 128, 128), 128)
            total = own[c, :, cols]
            for k in near:
                total = total + c_recv[c, k, :, cols].astype(f32)
            feature = (residual_ref[at, cols].astype(f32) + total).astype(bf16)
            feature_ref[at, cols] = feature
            feature = feature.astype(f32)
            scaled[:, cols] = (feature * gain[pl.ds(j, 1), :]).astype(bf16)
            return squares + feature * feature

        squares = lax.fori_loop(0, width // 128, finish, jnp.zeros((span, 128), f32))
        column = jnp.sum(squares, axis=1, keepdims=True)
        line = jnp.sum(jnp.where(diagonal, column, 0.0), axis=0, keepdims=True)
        sq_send[c] = jnp.broadcast_to(line, (8, 128))
        for k in range(1, n):
            send_sq(c, k).start()

        @pl.loop(1, n)
        def _(k):
            d_send[c, k] = jnp.dot(
                scaled[...], draft[k], preferred_element_type=f32
            ).astype(bf16)
            send_d(c, k).start()

        d_own[c] = jnp.dot(scaled[...], draft[0], preferred_element_type=f32)

    @pl.loop(0, chunks)
    def _(c):
        for k in range(1, n):
            send_sq(c, k).wait_recv()
            send_d(c, k).wait_recv()
        total = d_own[c]
        line = sq_send[c, 0:1, :]
        for k in range(1, n):
            total = total + d_recv[c, k].astype(f32)
            line = line + sq_recv[c, k, 0:1, :]
        column = jnp.sum(jnp.where(diagonal, line, 0.0), axis=1, keepdims=True)
        inverse = lax.rsqrt(column / (width * n) + epsilon)
        drafted = (total * inverse).astype(bf16)
        source = lax.broadcasted_iota(jnp.int32, (nodes, nodes), 0)
        for r in range(per):
            request = c * per + r
            chosen = (source == parents_ref[pl.ds(request, 1), :]).astype(f32).astype(bf16)
            moved = lax.dot_general(
                chosen,
                drafted[r * nodes : (r + 1) * nodes],
                (((0,), (0,)), ((), ())),
                preferred_element_type=f32,
            )
            to = pl.ds(pl.multiple_of(request * nodes, nodes), nodes)
            drafted_ref[to, :] = moved.astype(bf16)

    for k in range(1, n):
        send_t(k).wait_send()
        for c in range(chunks):
            for send in (send_b, send_s, send_d, send_sq):
                send(c, k).wait_send()
    for c in range(chunks):
        for k in near:
            send_q(c, k).wait_send()
            send_c(c, k).wait_send()
        if relay:
            for i in range(2):
                forward_q(c, i).wait_send()
                pass_c(c, i).wait_send()


def hand_over(feature_ref, drafted_ref, feature_out, drafted_out):
    feature_out[...] = feature_ref[...]
    drafted_out[...] = drafted_ref[...]


def shards(
    n,
    query_heads,
    queries,
    tree_states,
    cache_codes,
    cache_scales,
    bit_widths,
    page_table,
    lengths,
    parents,
    tree_mask,
    output_weight,
    residual,
    norm_gain,
    draft_weight,
):
    rows, width = queries.shape
    slots, kv_heads, _, page, hd = cache_codes.shape
    requests = lengths.shape[0]
    nodes = rows // requests
    groups = query_heads // kv_heads
    heads = width // hd
    chunks = 2 if requests % 2 == 0 else 1
    while requests // chunks * nodes > 128:
        chunks *= 2
    span = rows // chunks
    kv_dev = max(1, heads // groups)
    units = requests // chunks * kv_dev
    lanes = min(groups, heads) * nodes
    stat_rows = -(-2 * units // 8) * 8
    tree_rows = tree_states.shape[0]
    wire = jnp.bfloat16 if tree_rows % 16 == 0 else jnp.float32
    out_width = draft_weight.shape[1] // n
    f32, bf16 = jnp.float32, jnp.bfloat16
    dma = pltpu.SemaphoreType.DMA
    vmem, smem, hbm = (
        pl.BlockSpec(memory_space=space) for space in (pltpu.VMEM, pltpu.SMEM, pl.ANY)
    )
    sems = dma((2, chunks, n))
    results = pl.pallas_call(
        functools.partial(kernel, n, chunks, groups),
        out_shape=(
            jax.ShapeDtypeStruct((rows, width), bf16),
            jax.ShapeDtypeStruct((rows, out_width), bf16),
        ),
        in_specs=[vmem, vmem, vmem, smem, smem, smem, vmem, vmem, vmem, vmem, hbm, hbm, hbm],
        out_specs=(vmem, vmem),
        scratch_shapes=[
            pltpu.VMEM(cache_codes.shape, bf16),
            pltpu.VMEM((n, width, width), bf16),
            pltpu.VMEM((n, width, out_width), bf16),
            pltpu.VMEM((chunks, n, span, width), bf16),
            pltpu.VMEM((n, 2, tree_rows, kv_dev * hd), wire),
            pltpu.VMEM((2, rows, kv_dev * hd), wire),
            pltpu.VMEM((chunks, n, units, hd, lanes), bf16),
            pltpu.VMEM((chunks, n, units, hd, lanes), bf16),
            pltpu.VMEM((chunks, n, stat_rows, lanes), f32),
            pltpu.VMEM((chunks, n, stat_rows, lanes), f32),
            pltpu.VMEM((chunks, units, hd, lanes), f32),
            pltpu.VMEM((chunks, stat_rows, lanes), f32),
            pltpu.VMEM((span, width), bf16),
            pltpu.VMEM((chunks, n, span, width), bf16),
            pltpu.VMEM((chunks, n, span, width), bf16),
            pltpu.VMEM((chunks, span, width), f32),
            pltpu.VMEM((span, width), bf16),
            pltpu.VMEM((chunks, n, span, out_width), bf16),
            pltpu.VMEM((chunks, n, span, out_width), bf16),
            pltpu.VMEM((chunks, span, out_width), f32),
            pltpu.VMEM((chunks, 8, 128), f32),
            pltpu.VMEM((chunks, n, 8, 128), f32),
            pltpu.VMEM((width // 128, 128), f32),
            dma,
            dma((n,)),
            dma((n,)),
            sems,
            dma((2, n)),
            sems,
            sems,
            sems,
            sems,
            sems,
        ],
        compiler_params=pltpu.CompilerParams(
            collective_id=0, has_side_effects=True, vmem_limit_bytes=63 * 1024 * 1024
        ),
    )(
        queries,
        tree_states,
        cache_scales,
        bit_widths,
        page_table,
        lengths,
        parents,
        tree_mask,
        residual,
        norm_gain.reshape(-1, 128),
        cache_codes,
        output_weight,
        draft_weight,
    )
    return pl.pallas_call(
        hand_over,
        out_shape=tuple(jax.ShapeDtypeStruct(one.shape, one.dtype) for one in results),
        in_specs=[vmem, vmem],
        out_specs=(vmem, vmem),
        compiler_params=pltpu.CompilerParams(vmem_limit_bytes=63 * 1024 * 1024),
    )(*results)


def solution(mesh):
    n = mesh.shape["tensor"]
    placed = (
        P("dp", "tensor"),
        P(("dp", "tensor"), None),
        P(("dp", "tensor"), None, None, None, None),
        P(("dp", "tensor"), None, None, None),
        P("dp"),
        P("dp", None),
        P("dp"),
        P("dp", None),
        P("dp", None, None),
        P("tensor", None),
        P("dp", "tensor"),
        P("tensor"),
        P("tensor", None),
    )

    def run(*arrays):
        query_heads = arrays[0].shape[1] // arrays[2].shape[-1]
        return jax.shard_map(
            functools.partial(shards, n, query_heads),
            mesh=mesh,
            in_specs=placed,
            out_specs=(P("dp", "tensor"), P("dp", "tensor")),
            check_vma=False,
        )(*arrays)

    return run
```

```python
import functools
import math

import jax
import jax.numpy as jnp
from jax import lax
from jax.experimental import pallas as pl
from jax.experimental.pallas import tpu as pltpu
from jax.sharding import PartitionSpec as P

MESH = pl.DeviceIdType.MESH
masked_score = -1e30
epsilon = 1e-05


def attend(stacked, keys, values, live, scale):
    floor = masked_score / scale
    raw = lax.dot_general(
        keys, stacked, (((1,), (1,)), ((), ())), preferred_element_type=jnp.float32
    )
    raw = jnp.where(live, raw, floor)
    top = jnp.max(raw, axis=0, keepdims=True)
    base = jnp.where(top == floor, 0.0, top)
    weights = jnp.exp2((raw - base) * (scale * math.log2(math.e)))
    total = jnp.sum(weights, axis=0, keepdims=True)
    mixed = lax.dot_general(
        values,
        weights.astype(jnp.bfloat16),
        (((0,), (0,)), ((), ())),
        preferred_element_type=jnp.float32,
    )
    return top * scale, total, mixed * (1.0 / jnp.where(total > 0, total, 1.0))


def kernel(
    n,
    chunks,
    groups,
    q_ref,
    tree_ref,
    scales_ref,
    bits_ref,
    table_ref,
    lengths_ref,
    parents_ref,
    mask_ref,
    residual_ref,
    gain_ref,
    codes_hbm,
    weight_hbm,
    draft_hbm,
    feature_ref,
    drafted_ref,
    cache,
    weight,
    draft,
    q_all,
    t_send,
    t_all,
    b_send,
    b_recv,
    s_send,
    s_recv,
    t_out,
    t_stat,
    attended,
    c_send,
    c_recv,
    own,
    scaled,
    d_send,
    d_recv,
    d_own,
    sq_send,
    sq_recv,
    gain,
    local_sem,
    weight_sem,
    draft_sem,
    q_sems,
    t_sems,
    b_sems,
    s_sems,
    c_sems,
    d_sems,
    sq_sems,
):
    me = lax.axis_index("tensor")
    rows, width = q_ref.shape
    slots, kv_heads, _, page, hd = cache.shape
    requests = lengths_ref.shape[0]
    nodes = rows // requests
    per = requests // chunks
    span = per * nodes
    heads = width // hd
    gh = min(groups, heads)
    kv_dev = heads // gh
    pages = table_ref.shape[1] // n
    block = pages * page
    tree_rows = tree_ref.shape[0]
    tree_width = kv_dev * hd
    out_width = draft.shape[2]
    scale = 1.0 / math.sqrt(hd)
    lanes = gh * nodes
    f32, bf16 = jnp.float32, jnp.bfloat16

    relay = n == 4
    part_rows = span // 2
    part_units = b_send.shape[2] // 2

    def flipped(k):
        low = lax.rem(me + k, 2)
        return 2 * lax.rem(me // 2 + k // 2, 2) + low

    def ahead(k):
        return flipped(k) if relay else lax.rem(me + k, n)

    def behind(k):
        return flipped(k) if relay else lax.rem(me + n - k, n)

    def back(k):
        return k if relay else n - k

    def remote(src, dst, sems, index, k):
        return pltpu.make_async_remote_copy(
            src_ref=src,
            dst_ref=dst,
            send_sem=sems.at[(0, *index)],
            recv_sem=sems.at[(1, *index)],
            device_id={"tensor": ahead(k)},
            device_id_type=MESH,
        )

    def send_q(c, k):
        return remote(q_all.at[c, 0], q_all.at[c, k], q_sems, (c, k), k)

    def forward_q(c, i):
        rows_at = pl.ds(i * part_rows, part_rows)
        return remote(
            q_all.at[c, 1 + i, rows_at],
            q_all.at[c, 3, rows_at],
            q_sems,
            (c, 3 - 3 * i),
            2 - i,
        )

    def pass_c(c, i):
        rows_at = pl.ds(i * part_rows, part_rows)
        return remote(
            c_send.at[c, 3, rows_at], c_recv.at[c, 3, rows_at], c_sems, (c, 3 - 3 * i), 1 + i
        )

    def pass_b(c, i):
        at = pl.ds(i * part_units, part_units)
        return remote(
            b_send.at[c, 3, at], b_recv.at[c, 3, at], b_sems, (c, 3 - 3 * i), 1 + i
        )

    def pass_s(c, i):
        return remote(s_send.at[c, 3], s_recv.at[c, 3 - 3 * i], s_sems, (c, 3 - 3 * i), 1 + i)

    def send_t(k):
        at = pl.ds(pl.multiple_of(me * tree_rows, tree_rows), tree_rows)
        return remote(t_send.at[k], t_all.at[:, at, :], t_sems, (k,), k)

    def send_b(c, k):
        return remote(b_send.at[c, back(k)], b_recv.at[c, k], b_sems, (c, k), k)

    def send_s(c, k):
        return remote(s_send.at[c, back(k)], s_recv.at[c, k], s_sems, (c, k), k)

    def send_c(c, k):
        return remote(c_send.at[c, k], c_recv.at[c, k], c_sems, (c, k), k)

    def send_d(c, k):
        return remote(d_send.at[c, k], d_recv.at[c, k], d_sems, (c, k), k)

    def send_sq(c, k):
        return remote(sq_send.at[c], sq_recv.at[c, k], sq_sems, (c, k), k)

    def load_weight(k):
        at = pl.ds(pl.multiple_of(ahead(k) * width, width), width)
        return pltpu.make_async_copy(weight_hbm.at[:, at], weight.at[k], weight_sem.at[k])

    def load_draft(k):
        at = pl.ds(pl.multiple_of(ahead(k) * out_width, out_width), out_width)
        return pltpu.make_async_copy(draft_hbm.at[:, at], draft.at[k], draft_sem.at[k])

    load_cache = pltpu.make_async_copy(codes_hbm, cache, local_sem)
    load_cache.start()
    gain[...] = gain_ref[...].astype(f32)

    barrier = pltpu.get_barrier_semaphore()
    for k in range(1, n):
        pl.semaphore_signal(
            barrier, inc=1, device_id={"tensor": ahead(k)}, device_id_type=MESH
        )
    for c in range(chunks):
        q_all[c, 0] = q_ref[c * span : (c + 1) * span, :]
    for k in range(n):
        first = ahead(k) * heads // groups
        for part in range(2):
            at = pl.ds(pl.multiple_of((part * kv_heads + first) * hd, hd), tree_width)
            t_send[k, part] = tree_ref[:, at].astype(t_send.dtype)
    mine = pl.ds(pl.multiple_of(me * tree_rows, tree_rows), tree_rows)
    t_all[:, mine, :] = t_send[0]
    pl.semaphore_wait(barrier, n - 1)

    near = range(1, 3 if relay else n)
    for c in range(chunks):
        for k in near:
            send_q(c, k).start()
    for k in range(1, n):
        send_t(k).start()
    for k in range(n):
        load_weight(k).start()
    for k in range(n):
        load_draft(k).start()

    load_cache.wait()

    @pl.loop(0, slots)
    def _(slot):
        for g in range(0, kv_heads, 2):
            codes, results = cache[slot, g : g + 2].astype(f32), []
            for i in range(2):
                level = jnp.full((1, hd), jnp.left_shift(jnp.int32(1), bits_ref[g + i]), jnp.int32)
                level = level.astype(f32)
                ratio = scales_ref[slot, g + i] / level
                for part in range(2):
                    centred = 2.0 * codes[i, part] - (level - 1.0)
                    results.append((ratio[part : part + 1] * centred).astype(bf16))
            for i, result in enumerate(results):
                cache[slot, g + i // 2, i % 2] = result

    place = lax.broadcasted_iota(jnp.int32, (block, lanes), 0)

    def stack(c, k, r, j):
        at = slice(r * nodes, (r + 1) * nodes)
        cols = [slice((j * gh + h) * hd, (j * gh + h + 1) * hd) for h in range(gh)]
        return jnp.concatenate([q_all[c, k, at, col] for col in cols], axis=0)

    def receive_q(c):
        for k in (1, 2):
            send_q(c, k).wait_recv()
        for i in range(2):
            forward_q(c, i).start()

    def merge(c):
        for i in range(2):
            pass_b(c, i).wait_recv()
            pass_s(c, i).wait_recv()
            k = 2 - i
            for u in range(i * part_units, (i + 1) * part_units):
                row, below = slice(2 * u, 2 * u + 1), slice(2 * u + 1, 2 * u + 2)
                tops = s_send[c, k, row], s_recv[c, 3 - 3 * i, row]
                overall = jnp.maximum(*tops)
                first = jnp.exp(tops[0] - overall) * s_send[c, k, below]
                other = jnp.exp(tops[1] - overall) * s_recv[c, 3 - 3 * i, below]
                total = first + other
                inverse = 1.0 / jnp.where(total > 0, total, 1.0)
                mixed = (first * inverse) * b_send[c, k, u].astype(f32)
                mixed = mixed + (other * inverse) * b_recv[c, 3, u].astype(f32)
                b_send[c, k, u] = mixed.astype(bf16)
                s_send[c, k, row] = overall
                s_send[c, k, below] = total
            send_b(c, k).start()
            send_s(c, k).start()

    @pl.loop(0, chunks * n)
    def _(step):
        later = jnp.maximum(step - chunks, 0)
        own_step = step < chunks
        c = jnp.where(own_step, step, later // (n - 1))
        k = jnp.where(own_step, 0, 1 + lax.rem(later, n - 1))

        if n > 0:
            if relay:
                @pl.when(step == chunks)
                def _():
                    receive_q(0)

                @pl.when(k == 3)
                def _():
                    @pl.when(c < chunks - 1)
                    def _():
                        receive_q(c + 1)

                    @pl.when(c > 0)
                    def _():
                        merge(c - 1)

                    for i in range(2):
                        forward_q(c, i).wait_recv()
            else:
                @pl.when(k > 0)
                def _():
                    send_q(c, k).wait_recv()

            first = behind(k) * heads // groups
            for r in range(per):
                request = c * per + r
                ids = [table_ref[request, me * pages + p] for p in range(pages)]
                live = place < lengths_ref[request] - me * block
                for j in range(kv_dev):
                    u = r * kv_dev + j
                    keys, values = (
                        jnp.concatenate([cache[i, first + j, part] for i in ids], axis=0)
                        for part in range(2)
                    )
                    top, total, mixed = attend(stack(c, k, r, j), keys, values, live, scale)
                    s_send[c, k, 2 * u : 2 * u + 1, :] = top
                    s_send[c, k, 2 * u + 1 : 2 * u + 2, :] = total
                    b_send[c, k, u] = mixed.astype(bf16)

            if relay:
                @pl.when(k == 3)
                def _():
                    for i in range(2):
                        pass_b(c, i).start()
                        pass_s(c, i).start()
            else:
                @pl.when(k > 0)
                def _():
                    send_b(c, back(k)).start()
                    send_s(c, back(k)).start()

    for k in range(1, n):
        send_t(k).wait_recv()

    turn_row = lax.broadcasted_iota(jnp.int32, (nodes, lanes), 0)
    turn_lane = lax.broadcasted_iota(jnp.int32, (nodes, lanes), 1)
    turn = (turn_row == lax.rem(turn_lane, nodes)).astype(f32).astype(bf16)

    @pl.loop(0, chunks)
    def _(c):
        for r in range(per):
            request = c * per + r
            turned = lax.dot_general(
                mask_ref[request].astype(f32).astype(bf16),
                turn,
                (((0,), (0,)), ((), ())),
                preferred_element_type=f32,
            )
            at = pl.ds(pl.multiple_of(request * nodes, nodes), nodes)
            for j in range(kv_dev):
                u = r * kv_dev + j
                col = slice(j * hd, (j + 1) * hd)
                keys, values = (t_all[part, at, col].astype(bf16) for part in range(2))
                top, total, mixed = attend(stack(c, 0, r, j), keys, values, turned > 0.5, scale)
                t_stat[c, 2 * u : 2 * u + 1, :] = top
                t_stat[c, 2 * u + 1 : 2 * u + 2, :] = total
                t_out[c, u] = mixed

    if relay:
        merge(chunks - 1)

    for k in range(n):
        load_weight(k).wait()

    tile = min(width, 512)

    @pl.loop(0, chunks)
    def _(c):
        for k in near:
            send_b(c, k).wait_recv()
            send_s(c, k).wait_recv()
        for u in range(per * kv_dev):
            tops, totals = (
                [t_stat[c, row], s_send[c, 0, row]] + [s_recv[c, k, row] for k in near]
                for row in (slice(2 * u, 2 * u + 1), slice(2 * u + 1, 2 * u + 2))
            )
            overall = functools.reduce(jnp.maximum, tops)
            shares = [jnp.exp(one - overall) * total for one, total in zip(tops, totals)]
            inverse = 1.0 / functools.reduce(jnp.add, shares)
            blocks = [t_out[c, u], b_send[c, 0, u].astype(f32)]
            blocks += [b_recv[c, k, u].astype(f32) for k in near]
            mixed = functools.reduce(
                jnp.add, [one * inverse * b for one, b in zip(shares, blocks)]
            )
            mixed = mixed.T.astype(bf16)
            r, j = u // kv_dev, u % kv_dev
            for h in range(gh):
                attended[
                    r * nodes : (r + 1) * nodes,
                    (j * gh + h) * hd : (j * gh + h + 1) * hd,
                ] = mixed[h * nodes : (h + 1) * nodes]

        def project(k, store):
            @pl.loop(0, width // tile)
            def _(j):
                cols = pl.ds(pl.multiple_of(j * tile, tile), tile)
                store(
                    cols,
                    jnp.dot(attended[...], weight[k, :, cols], preferred_element_type=f32),
                )

        def store_own(cols, product):
            own[c, :, cols] = product

        def store_send(k, cols, product):
            c_send[c, k, :, cols] = product.astype(bf16)

        def store_joined(k, cols, product):
            i = 2 - k
            lower = slice(i * part_rows, (i + 1) * part_rows)
            upper = slice((1 - i) * part_rows, (2 - i) * part_rows)
            passed = c_recv[c, 3, lower, cols].astype(f32)
            c_send[c, k, lower, cols] = (product[lower] + passed).astype(bf16)
            c_send[c, k, upper, cols] = product[upper].astype(bf16)

        if relay:
            project(3, functools.partial(store_send, 3))
            for i in range(2):
                pass_c(c, i).start()
            project(0, store_own)
            for k in (1, 2):
                pass_c(c, 2 - k).wait_recv()
                project(k, functools.partial(store_joined, k))
                send_c(c, k).start()
        else:
            @pl.loop(1, n)
            def _(k):
                project(k, functools.partial(store_send, k))
                send_c(c, k).start()

            project(0, store_own)

    for k in range(n):
        load_draft(k).wait()

    row_of = lax.broadcasted_iota(jnp.int32, (span, 128), 0)
    lane_of = lax.broadcasted_iota(jnp.int32, (span, 128), 1)
    diagonal = row_of == lane_of

    @pl.loop(0, chunks)
    def _(c):
        for k in near:
            send_c(c, k).wait_recv()
        at = pl.ds(pl.multiple_of(c * span, span), span)

        def finish(j, squares):
            cols = pl.ds(pl.multiple_of(j * 128, 128), 128)
            total = own[c, :, cols]
            for k in near:
                total = total + c_recv[c, k, :, cols].astype(f32)
            feature = (residual_ref[at, cols].astype(f32) + total).astype(bf16)
            feature_ref[at, cols] = feature
            feature = feature.astype(f32)
            scaled[:, cols] = (feature * gain[pl.ds(j, 1), :]).astype(bf16)
            return squares + feature * feature

        squares = lax.fori_loop(0, width // 128, finish, jnp.zeros((span, 128), f32))
        column = jnp.sum(squares, axis=1, keepdims=True)
        line = jnp.sum(jnp.where(diagonal, column, 0.0), axis=0, keepdims=True)
        sq_send[c] = jnp.broadcast_to(line, (8, 128))
        for k in range(1, n):
            send_sq(c, k).start()

        @pl.loop(1, n)
        def _(k):
            d_send[c, k] = jnp.dot(
                scaled[...], draft[k], preferred_element_type=f32
            ).astype(bf16)
            send_d(c, k).start()

        d_own[c] = jnp.dot(scaled[...], draft[0], preferred_element_type=f32)

    @pl.loop(0, chunks)
    def _(c):
        for k in range(1, n):
            send_sq(c, k).wait_recv()
            send_d(c, k).wait_recv()
        total = d_own[c]
        line = sq_send[c, 0:1, :]
        for k in range(1, n):
            total = total + d_recv[c, k].astype(f32)
            line = line + sq_recv[c, k, 0:1, :]
        column = jnp.sum(jnp.where(diagonal, line, 0.0), axis=1, keepdims=True)
        inverse = lax.rsqrt(column / (width * n) + epsilon)
        drafted = (total * inverse).astype(bf16)
        source = lax.broadcasted_iota(jnp.int32, (nodes, nodes), 0)
        for r in range(per):
            request = c * per + r
            chosen = (source == parents_ref[pl.ds(request, 1), :]).astype(f32).astype(bf16)
            moved = lax.dot_general(
                chosen,
                drafted[r * nodes : (r + 1) * nodes],
                (((0,), (0,)), ((), ())),
                preferred_element_type=f32,
            )
            to = pl.ds(pl.multiple_of(request * nodes, nodes), nodes)
            drafted_ref[to, :] = moved.astype(bf16)

    for k in range(1, n):
        send_t(k).wait_send()
        for c in range(chunks):
            for send in (send_d, send_sq):
                send(c, k).wait_send()
    for c in range(chunks):
        for k in near:
            for send in (send_q, send_b, send_s, send_c):
                send(c, k).wait_send()
        if relay:
            for i in range(2):
                forward_q(c, i).wait_send()
                pass_b(c, i).wait_send()
                pass_s(c, i).wait_send()
                pass_c(c, i).wait_send()


def hand_over(feature_ref, drafted_ref, feature_out, drafted_out):
    feature_out[...] = feature_ref[...]
    drafted_out[...] = drafted_ref[...]


def shards(
    n,
    query_heads,
    queries,
    tree_states,
    cache_codes,
    cache_scales,
    bit_widths,
    page_table,
    lengths,
    parents,
    tree_mask,
    output_weight,
    residual,
    norm_gain,
    draft_weight,
):
    rows, width = queries.shape
    slots, kv_heads, _, page, hd = cache_codes.shape
    requests = lengths.shape[0]
    nodes = rows // requests
    groups = query_heads // kv_heads
    heads = width // hd
    chunks = 2 if requests % 2 == 0 else 1
    while requests // chunks * nodes > 128:
        chunks *= 2
    span = rows // chunks
    kv_dev = max(1, heads // groups)
    units = requests // chunks * kv_dev
    lanes = min(groups, heads) * nodes
    stat_rows = -(-2 * units // 8) * 8
    tree_rows = tree_states.shape[0]
    wire = jnp.bfloat16 if tree_rows % 16 == 0 else jnp.float32
    out_width = draft_weight.shape[1] // n
    f32, bf16 = jnp.float32, jnp.bfloat16
    dma = pltpu.SemaphoreType.DMA
    vmem, smem, hbm = (
        pl.BlockSpec(memory_space=space) for space in (pltpu.VMEM, pltpu.SMEM, pl.ANY)
    )
    sems = dma((2, chunks, n))
    results = pl.pallas_call(
        functools.partial(kernel, n, chunks, groups),
        out_shape=(
            jax.ShapeDtypeStruct((rows, width), bf16),
            jax.ShapeDtypeStruct((rows, out_width), bf16),
        ),
        in_specs=[vmem, vmem, vmem, smem, smem, smem, vmem, vmem, vmem, vmem, hbm, hbm, hbm],
        out_specs=(vmem, vmem),
        scratch_shapes=[
            pltpu.VMEM(cache_codes.shape, bf16),
            pltpu.VMEM((n, width, width), bf16),
            pltpu.VMEM((n, width, out_width), bf16),
            pltpu.VMEM((chunks, n, span, width), bf16),
            pltpu.VMEM((n, 2, tree_rows, kv_dev * hd), wire),
            pltpu.VMEM((2, rows, kv_dev * hd), wire),
            pltpu.VMEM((chunks, n, units, hd, lanes), bf16),
            pltpu.VMEM((chunks, n, units, hd, lanes), bf16),
            pltpu.VMEM((chunks, n, stat_rows, lanes), f32),
            pltpu.VMEM((chunks, n, stat_rows, lanes), f32),
            pltpu.VMEM((chunks, units, hd, lanes), f32),
            pltpu.VMEM((chunks, stat_rows, lanes), f32),
            pltpu.VMEM((span, width), bf16),
            pltpu.VMEM((chunks, n, span, width), bf16),
            pltpu.VMEM((chunks, n, span, width), bf16),
            pltpu.VMEM((chunks, span, width), f32),
            pltpu.VMEM((span, width), bf16),
            pltpu.VMEM((chunks, n, span, out_width), bf16),
            pltpu.VMEM((chunks, n, span, out_width), bf16),
            pltpu.VMEM((chunks, span, out_width), f32),
            pltpu.VMEM((chunks, 8, 128), f32),
            pltpu.VMEM((chunks, n, 8, 128), f32),
            pltpu.VMEM((width // 128, 128), f32),
            dma,
            dma((n,)),
            dma((n,)),
            sems,
            dma((2, n)),
            sems,
            sems,
            sems,
            sems,
            sems,
        ],
        compiler_params=pltpu.CompilerParams(
            collective_id=0, has_side_effects=True, vmem_limit_bytes=63 * 1024 * 1024
        ),
    )(
        queries,
        tree_states,
        cache_scales,
        bit_widths,
        page_table,
        lengths,
        parents,
        tree_mask,
        residual,
        norm_gain.reshape(-1, 128),
        cache_codes,
        output_weight,
        draft_weight,
    )
    return pl.pallas_call(
        hand_over,
        out_shape=tuple(jax.ShapeDtypeStruct(one.shape, one.dtype) for one in results),
        in_specs=[vmem, vmem],
        out_specs=(vmem, vmem),
        compiler_params=pltpu.CompilerParams(vmem_limit_bytes=63 * 1024 * 1024),
    )(*results)


def solution(mesh):
    n = mesh.shape["tensor"]
    placed = (
        P("dp", "tensor"),
        P(("dp", "tensor"), None),
        P(("dp", "tensor"), None, None, None, None),
        P(("dp", "tensor"), None, None, None),
        P("dp"),
        P("dp", None),
        P("dp"),
        P("dp", None),
        P("dp", None, None),
        P("tensor", None),
        P("dp", "tensor"),
        P("tensor"),
        P("tensor", None),
    )

    def run(*arrays):
        query_heads = arrays[0].shape[1] // arrays[2].shape[-1]
        return jax.shard_map(
            functools.partial(shards, n, query_heads),
            mesh=mesh,
            in_specs=placed,
            out_specs=(P("dp", "tensor"), P("dp", "tensor")),
            check_vma=False,
        )(*arrays)

    return run
```

```python
import functools
import math

import jax
import jax.numpy as jnp
from jax import lax
from jax.experimental import pallas as pl
from jax.experimental.pallas import tpu as pltpu
from jax.sharding import PartitionSpec as P

MESH = pl.DeviceIdType.MESH
masked_score = -1e30
epsilon = 1e-05


def attend(stacked, keys, values, live, scale):
    floor = masked_score / scale
    raw = lax.dot_general(
        keys, stacked, (((1,), (1,)), ((), ())), preferred_element_type=jnp.float32
    )
    raw = jnp.where(live, raw, floor)
    top = jnp.max(raw, axis=0, keepdims=True)
    base = jnp.where(top == floor, 0.0, top)
    weights = jnp.exp2((raw - base) * (scale * math.log2(math.e)))
    total = jnp.sum(weights, axis=0, keepdims=True)
    mixed = lax.dot_general(
        values,
        weights.astype(jnp.bfloat16),
        (((0,), (0,)), ((), ())),
        preferred_element_type=jnp.float32,
    )
    return top * scale, total, mixed * (1.0 / jnp.where(total > 0, total, 1.0))


def kernel(
    n,
    chunks,
    groups,
    q_ref,
    tree_ref,
    scales_ref,
    bits_ref,
    table_ref,
    lengths_ref,
    parents_ref,
    mask_ref,
    residual_ref,
    gain_ref,
    codes_hbm,
    weight_hbm,
    draft_hbm,
    feature_ref,
    drafted_ref,
    cache,
    weight,
    draft,
    q_all,
    t_send,
    t_all,
    b_send,
    b_recv,
    s_send,
    s_recv,
    t_out,
    t_stat,
    attended,
    c_send,
    c_recv,
    own,
    scaled,
    d_send,
    d_recv,
    d_own,
    sq_send,
    sq_recv,
    gain,
    local_sem,
    weight_sem,
    draft_sem,
    q_sems,
    t_sems,
    b_sems,
    s_sems,
    c_sems,
    d_sems,
    sq_sems,
):
    me = lax.axis_index("tensor")
    rows, width = q_ref.shape
    slots, kv_heads, _, page, hd = cache.shape
    requests = lengths_ref.shape[0]
    nodes = rows // requests
    per = requests // chunks
    span = per * nodes
    heads = width // hd
    gh = min(groups, heads)
    kv_dev = heads // gh
    pages = table_ref.shape[1] // n
    block = pages * page
    tree_rows = tree_ref.shape[0]
    tree_width = kv_dev * hd
    out_width = draft.shape[2]
    scale = 1.0 / math.sqrt(hd)
    lanes = gh * nodes
    f32, bf16 = jnp.float32, jnp.bfloat16

    relay = n == 4
    part_rows = span // 2
    part_units = b_send.shape[2] // 2

    def flipped(k):
        low = lax.rem(me + k, 2)
        return 2 * lax.rem(me // 2 + k // 2, 2) + low

    def ahead(k):
        return flipped(k) if relay else lax.rem(me + k, n)

    def behind(k):
        return flipped(k) if relay else lax.rem(me + n - k, n)

    def back(k):
        return k if relay else n - k

    def remote(src, dst, sems, index, k):
        return pltpu.make_async_remote_copy(
            src_ref=src,
            dst_ref=dst,
            send_sem=sems.at[(0, *index)],
            recv_sem=sems.at[(1, *index)],
            device_id={"tensor": ahead(k)},
            device_id_type=MESH,
        )

    def send_q(c, k):
        return remote(q_all.at[c, 0], q_all.at[c, k], q_sems, (c, k), k)

    def forward_q(c, i):
        rows_at = pl.ds(i * part_rows, part_rows)
        return remote(
            q_all.at[c, 1 + i, rows_at],
            q_all.at[c, 3, rows_at],
            q_sems,
            (c, 3 - 3 * i),
            2 - i,
        )

    def pass_c(c, i):
        rows_at = pl.ds(i * part_rows, part_rows)
        return remote(
            c_send.at[c, 3, rows_at], c_recv.at[c, 3, rows_at], c_sems, (c, 3 - 3 * i), 1 + i
        )

    def pass_b(c, i):
        at = pl.ds(i * part_units, part_units)
        return remote(
            b_send.at[c, 3, at], b_recv.at[c, 3, at], b_sems, (c, 3 - 3 * i), 1 + i
        )

    def pass_s(c, i):
        return remote(s_send.at[c, 3], s_recv.at[c, 3 - 3 * i], s_sems, (c, 3 - 3 * i), 1 + i)

    def send_t(k):
        at = pl.ds(pl.multiple_of(me * tree_rows, tree_rows), tree_rows)
        return remote(t_send.at[k], t_all.at[:, at, :], t_sems, (k,), k)

    def send_b(c, k):
        return remote(b_send.at[c, back(k)], b_recv.at[c, k], b_sems, (c, k), k)

    def send_s(c, k):
        return remote(s_send.at[c, back(k)], s_recv.at[c, k], s_sems, (c, k), k)

    def send_c(c, k):
        return remote(c_send.at[c, k], c_recv.at[c, k], c_sems, (c, k), k)

    def send_d(c, k):
        return remote(d_send.at[c, k], d_recv.at[c, k], d_sems, (c, k), k)

    def send_sq(c, k):
        return remote(sq_send.at[c], sq_recv.at[c, k], sq_sems, (c, k), k)

    def load_weight(k):
        at = pl.ds(pl.multiple_of(ahead(k) * width, width), width)
        return pltpu.make_async_copy(weight_hbm.at[:, at], weight.at[k], weight_sem.at[k])

    def load_draft(k):
        at = pl.ds(pl.multiple_of(ahead(k) * out_width, out_width), out_width)
        return pltpu.make_async_copy(draft_hbm.at[:, at], draft.at[k], draft_sem.at[k])

    load_cache = pltpu.make_async_copy(codes_hbm, cache, local_sem)
    load_cache.start()
    gain[...] = gain_ref[...].astype(f32)

    barrier = pltpu.get_barrier_semaphore()
    for k in range(1, n):
        pl.semaphore_signal(
            barrier, inc=1, device_id={"tensor": ahead(k)}, device_id_type=MESH
        )
    for c in range(chunks):
        q_all[c, 0] = q_ref[c * span : (c + 1) * span, :]
    for k in range(n):
        first = ahead(k) * heads // groups
        for part in range(2):
            at = pl.ds(pl.multiple_of((part * kv_heads + first) * hd, hd), tree_width)
            t_send[k, part] = tree_ref[:, at].astype(t_send.dtype)
    mine = pl.ds(pl.multiple_of(me * tree_rows, tree_rows), tree_rows)
    t_all[:, mine, :] = t_send[0]
    pl.semaphore_wait(barrier, n - 1)

    near = range(1, 3 if relay else n)
    for k in near:
        send_q(0, k).start()
    for k in range(n):
        load_weight(k).start()
    for k in range(n):
        load_draft(k).start()

    load_cache.wait()

    @pl.loop(0, slots)
    def _(slot):
        for g in range(0, kv_heads, 2):
            codes, results = cache[slot, g : g + 2].astype(f32), []
            for i in range(2):
                level = jnp.full((1, hd), jnp.left_shift(jnp.int32(1), bits_ref[g + i]), jnp.int32)
                level = level.astype(f32)
                ratio = scales_ref[slot, g + i] / level
                for part in range(2):
                    centred = 2.0 * codes[i, part] - (level - 1.0)
                    results.append((ratio[part : part + 1] * centred).astype(bf16))
            for i, result in enumerate(results):
                cache[slot, g + i // 2, i % 2] = result

    for c in range(1, chunks):
        for k in near:
            send_q(c, k).start()
    for k in range(1, n):
        send_t(k).start()

    place = lax.broadcasted_iota(jnp.int32, (block, lanes), 0)

    def stack(c, k, r, j):
        at = slice(r * nodes, (r + 1) * nodes)
        cols = [slice((j * gh + h) * hd, (j * gh + h + 1) * hd) for h in range(gh)]
        return jnp.concatenate([q_all[c, k, at, col] for col in cols], axis=0)

    def receive_q(c):
        for k in (1, 2):
            send_q(c, k).wait_recv()
        for i in range(2):
            forward_q(c, i).start()

    def merge(c):
        for i in range(2):
            pass_b(c, i).wait_recv()
            pass_s(c, i).wait_recv()
            k = 2 - i
            for u in range(i * part_units, (i + 1) * part_units):
                row, below = slice(2 * u, 2 * u + 1), slice(2 * u + 1, 2 * u + 2)
                tops = s_send[c, k, row], s_recv[c, 3 - 3 * i, row]
                overall = jnp.maximum(*tops)
                first = jnp.exp(tops[0] - overall) * s_send[c, k, below]
                other = jnp.exp(tops[1] - overall) * s_recv[c, 3 - 3 * i, below]
                total = first + other
                inverse = 1.0 / jnp.where(total > 0, total, 1.0)
                mixed = (first * inverse) * b_send[c, k, u].astype(f32)
                mixed = mixed + (other * inverse) * b_recv[c, 3, u].astype(f32)
                b_send[c, k, u] = mixed.astype(bf16)
                s_send[c, k, row] = overall
                s_send[c, k, below] = total
            send_b(c, k).start()
            send_s(c, k).start()

    @pl.loop(0, chunks * n)
    def _(step):
        later = jnp.maximum(step - chunks, 0)
        own_step = step < chunks
        c = jnp.where(own_step, step, later // (n - 1))
        k = jnp.where(own_step, 0, 1 + lax.rem(later, n - 1))

        if n > 0:
            if relay:
                @pl.when(step == 1)
                def _():
                    receive_q(0)

                @pl.when((k == 2) & (c < chunks - 1))
                def _():
                    receive_q(c + 1)

                @pl.when(k == 3)
                def _():
                    @pl.when(c > 0)
                    def _():
                        merge(c - 1)

                    for i in range(2):
                        forward_q(c, i).wait_recv()
            else:
                @pl.when(k > 0)
                def _():
                    send_q(c, k).wait_recv()

            first = behind(k) * heads // groups
            for r in range(per):
                request = c * per + r
                ids = [table_ref[request, me * pages + p] for p in range(pages)]
                live = place < lengths_ref[request] - me * block
                for j in range(kv_dev):
                    u = r * kv_dev + j
                    keys, values = (
                        jnp.concatenate([cache[i, first + j, part] for i in ids], axis=0)
                        for part in range(2)
                    )
                    top, total, mixed = attend(stack(c, k, r, j), keys, values, live, scale)
                    s_send[c, k, 2 * u : 2 * u + 1, :] = top
                    s_send[c, k, 2 * u + 1 : 2 * u + 2, :] = total
                    b_send[c, k, u] = mixed.astype(bf16)

            if relay:
                @pl.when(k == 3)
                def _():
                    for i in range(2):
                        pass_b(c, i).start()
                        pass_s(c, i).start()
            else:
                @pl.when(k > 0)
                def _():
                    send_b(c, back(k)).start()
                    send_s(c, back(k)).start()

    for k in range(1, n):
        send_t(k).wait_recv()

    turn_row = lax.broadcasted_iota(jnp.int32, (nodes, lanes), 0)
    turn_lane = lax.broadcasted_iota(jnp.int32, (nodes, lanes), 1)
    turn = (turn_row == lax.rem(turn_lane, nodes)).astype(f32).astype(bf16)

    @pl.loop(0, chunks)
    def _(c):
        for r in range(per):
            request = c * per + r
            turned = lax.dot_general(
                mask_ref[request].astype(f32).astype(bf16),
                turn,
                (((0,), (0,)), ((), ())),
                preferred_element_type=f32,
            )
            at = pl.ds(pl.multiple_of(request * nodes, nodes), nodes)
            for j in range(kv_dev):
                u = r * kv_dev + j
                col = slice(j * hd, (j + 1) * hd)
                keys, values = (t_all[part, at, col].astype(bf16) for part in range(2))
                top, total, mixed = attend(stack(c, 0, r, j), keys, values, turned > 0.5, scale)
                t_stat[c, 2 * u : 2 * u + 1, :] = top
                t_stat[c, 2 * u + 1 : 2 * u + 2, :] = total
                t_out[c, u] = mixed

    if relay:
        merge(chunks - 1)

    for k in range(n):
        load_weight(k).wait()

    tile = min(width, 512)

    @pl.loop(0, chunks)
    def _(c):
        for k in near:
            send_b(c, k).wait_recv()
            send_s(c, k).wait_recv()
        for u in range(per * kv_dev):
            tops, totals = (
                [t_stat[c, row], s_send[c, 0, row]] + [s_recv[c, k, row] for k in near]
                for row in (slice(2 * u, 2 * u + 1), slice(2 * u + 1, 2 * u + 2))
            )
            overall = functools.reduce(jnp.maximum, tops)
            shares = [jnp.exp(one - overall) * total for one, total in zip(tops, totals)]
            inverse = 1.0 / functools.reduce(jnp.add, shares)
            blocks = [t_out[c, u], b_send[c, 0, u].astype(f32)]
            blocks += [b_recv[c, k, u].astype(f32) for k in near]
            mixed = functools.reduce(
                jnp.add, [one * inverse * b for one, b in zip(shares, blocks)]
            )
            mixed = mixed.T.astype(bf16)
            r, j = u // kv_dev, u % kv_dev
            for h in range(gh):
                attended[
                    r * nodes : (r + 1) * nodes,
                    (j * gh + h) * hd : (j * gh + h + 1) * hd,
                ] = mixed[h * nodes : (h + 1) * nodes]

        def project(k, store):
            @pl.loop(0, width // tile)
            def _(j):
                cols = pl.ds(pl.multiple_of(j * tile, tile), tile)
                store(
                    cols,
                    jnp.dot(attended[...], weight[k, :, cols], preferred_element_type=f32),
                )

        def store_own(cols, product):
            own[c, :, cols] = product

        def store_send(k, cols, product):
            c_send[c, k, :, cols] = product.astype(bf16)

        def store_joined(k, cols, product):
            i = 2 - k
            lower = slice(i * part_rows, (i + 1) * part_rows)
            upper = slice((1 - i) * part_rows, (2 - i) * part_rows)
            passed = c_recv[c, 3, lower, cols].astype(f32)
            c_send[c, k, lower, cols] = (product[lower] + passed).astype(bf16)
            c_send[c, k, upper, cols] = product[upper].astype(bf16)

        if relay:
            project(3, functools.partial(store_send, 3))
            for i in range(2):
                pass_c(c, i).start()
            project(0, store_own)
            for k in (1, 2):
                pass_c(c, 2 - k).wait_recv()
                project(k, functools.partial(store_joined, k))
                send_c(c, k).start()
        else:
            @pl.loop(1, n)
            def _(k):
                project(k, functools.partial(store_send, k))
                send_c(c, k).start()

            project(0, store_own)

    for k in range(n):
        load_draft(k).wait()

    row_of = lax.broadcasted_iota(jnp.int32, (span, 128), 0)
    lane_of = lax.broadcasted_iota(jnp.int32, (span, 128), 1)
    diagonal = row_of == lane_of

    @pl.loop(0, chunks)
    def _(c):
        for k in near:
            send_c(c, k).wait_recv()
        at = pl.ds(pl.multiple_of(c * span, span), span)

        def finish(j, squares):
            cols = pl.ds(pl.multiple_of(j * 128, 128), 128)
            total = own[c, :, cols]
            for k in near:
                total = total + c_recv[c, k, :, cols].astype(f32)
            feature = (residual_ref[at, cols].astype(f32) + total).astype(bf16)
            feature_ref[at, cols] = feature
            feature = feature.astype(f32)
            scaled[:, cols] = (feature * gain[pl.ds(j, 1), :]).astype(bf16)
            return squares + feature * feature

        squares = lax.fori_loop(0, width // 128, finish, jnp.zeros((span, 128), f32))
        column = jnp.sum(squares, axis=1, keepdims=True)
        line = jnp.sum(jnp.where(diagonal, column, 0.0), axis=0, keepdims=True)
        sq_send[c] = jnp.broadcast_to(line, (8, 128))
        for k in range(1, n):
            send_sq(c, k).start()

        @pl.loop(1, n)
        def _(k):
            d_send[c, k] = jnp.dot(
                scaled[...], draft[k], preferred_element_type=f32
            ).astype(bf16)
            send_d(c, k).start()

        d_own[c] = jnp.dot(scaled[...], draft[0], preferred_element_type=f32)

    @pl.loop(0, chunks)
    def _(c):
        for k in range(1, n):
            send_sq(c, k).wait_recv()
            send_d(c, k).wait_recv()
        total = d_own[c]
        line = sq_send[c, 0:1, :]
        for k in range(1, n):
            total = total + d_recv[c, k].astype(f32)
            line = line + sq_recv[c, k, 0:1, :]
        column = jnp.sum(jnp.where(diagonal, line, 0.0), axis=1, keepdims=True)
        inverse = lax.rsqrt(column / (width * n) + epsilon)
        drafted = (total * inverse).astype(bf16)
        source = lax.broadcasted_iota(jnp.int32, (nodes, nodes), 0)
        for r in range(per):
            request = c * per + r
            chosen = (source == parents_ref[pl.ds(request, 1), :]).astype(f32).astype(bf16)
            moved = lax.dot_general(
                chosen,
                drafted[r * nodes : (r + 1) * nodes],
                (((0,), (0,)), ((), ())),
                preferred_element_type=f32,
            )
            to = pl.ds(pl.multiple_of(request * nodes, nodes), nodes)
            drafted_ref[to, :] = moved.astype(bf16)

    for k in range(1, n):
        send_t(k).wait_send()
        for c in range(chunks):
            for send in (send_d, send_sq):
                send(c, k).wait_send()
    for c in range(chunks):
        for k in near:
            for send in (send_q, send_b, send_s, send_c):
                send(c, k).wait_send()
        if relay:
            for i in range(2):
                forward_q(c, i).wait_send()
                pass_b(c, i).wait_send()
                pass_s(c, i).wait_send()
                pass_c(c, i).wait_send()


def hand_over(feature_ref, drafted_ref, feature_out, drafted_out):
    feature_out[...] = feature_ref[...]
    drafted_out[...] = drafted_ref[...]


def shards(
    n,
    query_heads,
    queries,
    tree_states,
    cache_codes,
    cache_scales,
    bit_widths,
    page_table,
    lengths,
    parents,
    tree_mask,
    output_weight,
    residual,
    norm_gain,
    draft_weight,
):
    rows, width = queries.shape
    slots, kv_heads, _, page, hd = cache_codes.shape
    requests = lengths.shape[0]
    nodes = rows // requests
    groups = query_heads // kv_heads
    heads = width // hd
    chunks = 2 if requests % 2 == 0 else 1
    while requests // chunks * nodes > 128:
        chunks *= 2
    span = rows // chunks
    kv_dev = max(1, heads // groups)
    units = requests // chunks * kv_dev
    lanes = min(groups, heads) * nodes
    stat_rows = -(-2 * units // 8) * 8
    tree_rows = tree_states.shape[0]
    wire = jnp.bfloat16 if tree_rows % 16 == 0 else jnp.float32
    out_width = draft_weight.shape[1] // n
    f32, bf16 = jnp.float32, jnp.bfloat16
    dma = pltpu.SemaphoreType.DMA
    vmem, smem, hbm = (
        pl.BlockSpec(memory_space=space) for space in (pltpu.VMEM, pltpu.SMEM, pl.ANY)
    )
    sems = dma((2, chunks, n))
    results = pl.pallas_call(
        functools.partial(kernel, n, chunks, groups),
        out_shape=(
            jax.ShapeDtypeStruct((rows, width), bf16),
            jax.ShapeDtypeStruct((rows, out_width), bf16),
        ),
        in_specs=[vmem, vmem, vmem, smem, smem, smem, vmem, vmem, vmem, vmem, hbm, hbm, hbm],
        out_specs=(vmem, vmem),
        scratch_shapes=[
            pltpu.VMEM(cache_codes.shape, bf16),
            pltpu.VMEM((n, width, width), bf16),
            pltpu.VMEM((n, width, out_width), bf16),
            pltpu.VMEM((chunks, n, span, width), bf16),
            pltpu.VMEM((n, 2, tree_rows, kv_dev * hd), wire),
            pltpu.VMEM((2, rows, kv_dev * hd), wire),
            pltpu.VMEM((chunks, n, units, hd, lanes), bf16),
            pltpu.VMEM((chunks, n, units, hd, lanes), bf16),
            pltpu.VMEM((chunks, n, stat_rows, lanes), f32),
            pltpu.VMEM((chunks, n, stat_rows, lanes), f32),
            pltpu.VMEM((chunks, units, hd, lanes), f32),
            pltpu.VMEM((chunks, stat_rows, lanes), f32),
            pltpu.VMEM((span, width), bf16),
            pltpu.VMEM((chunks, n, span, width), bf16),
            pltpu.VMEM((chunks, n, span, width), bf16),
            pltpu.VMEM((chunks, span, width), f32),
            pltpu.VMEM((span, width), bf16),
            pltpu.VMEM((chunks, n, span, out_width), bf16),
            pltpu.VMEM((chunks, n, span, out_width), bf16),
            pltpu.VMEM((chunks, span, out_width), f32),
            pltpu.VMEM((chunks, 8, 128), f32),
            pltpu.VMEM((chunks, n, 8, 128), f32),
            pltpu.VMEM((width // 128, 128), f32),
            dma,
            dma((n,)),
            dma((n,)),
            sems,
            dma((2, n)),
            sems,
            sems,
            sems,
            sems,
            sems,
        ],
        compiler_params=pltpu.CompilerParams(
            collective_id=0, has_side_effects=True, vmem_limit_bytes=63 * 1024 * 1024
        ),
    )(
        queries,
        tree_states,
        cache_scales,
        bit_widths,
        page_table,
        lengths,
        parents,
        tree_mask,
        residual,
        norm_gain.reshape(-1, 128),
        cache_codes,
        output_weight,
        draft_weight,
    )
    return pl.pallas_call(
        hand_over,
        out_shape=tuple(jax.ShapeDtypeStruct(one.shape, one.dtype) for one in results),
        in_specs=[vmem, vmem],
        out_specs=(vmem, vmem),
        compiler_params=pltpu.CompilerParams(vmem_limit_bytes=63 * 1024 * 1024),
    )(*results)


def solution(mesh):
    n = mesh.shape["tensor"]
    placed = (
        P("dp", "tensor"),
        P(("dp", "tensor"), None),
        P(("dp", "tensor"), None, None, None, None),
        P(("dp", "tensor"), None, None, None),
        P("dp"),
        P("dp", None),
        P("dp"),
        P("dp", None),
        P("dp", None, None),
        P("tensor", None),
        P("dp", "tensor"),
        P("tensor"),
        P("tensor", None),
    )

    def run(*arrays):
        query_heads = arrays[0].shape[1] // arrays[2].shape[-1]
        return jax.shard_map(
            functools.partial(shards, n, query_heads),
            mesh=mesh,
            in_specs=placed,
            out_specs=(P("dp", "tensor"), P("dp", "tensor")),
            check_vma=False,
        )(*arrays)

    return run
```

```python
import functools
import math

import jax
import jax.numpy as jnp
from jax import lax
from jax.experimental import pallas as pl
from jax.experimental.pallas import tpu as pltpu
from jax.sharding import PartitionSpec as P

MESH = pl.DeviceIdType.MESH
masked_score = -1e30
epsilon = 1e-05


def attend(stacked, keys, values, live, scale):
    floor = masked_score / scale
    raw = lax.dot_general(
        keys, stacked, (((1,), (1,)), ((), ())), preferred_element_type=jnp.float32
    )
    raw = jnp.where(live, raw, floor)
    top = jnp.max(raw, axis=0, keepdims=True)
    base = jnp.where(top == floor, 0.0, top)
    weights = jnp.exp2((raw - base) * (scale * math.log2(math.e)))
    total = jnp.sum(weights, axis=0, keepdims=True)
    mixed = lax.dot_general(
        values,
        weights.astype(jnp.bfloat16),
        (((0,), (0,)), ((), ())),
        preferred_element_type=jnp.float32,
    )
    return top * scale, total, mixed * (1.0 / jnp.where(total > 0, total, 1.0))


def kernel(
    n,
    chunks,
    groups,
    q_ref,
    tree_ref,
    scales_ref,
    bits_ref,
    table_ref,
    lengths_ref,
    parents_ref,
    mask_ref,
    residual_ref,
    gain_ref,
    codes_hbm,
    weight_hbm,
    draft_hbm,
    feature_ref,
    drafted_ref,
    cache,
    weight,
    draft,
    q_all,
    t_send,
    t_all,
    b_send,
    b_recv,
    s_send,
    s_recv,
    t_out,
    t_stat,
    attended,
    c_send,
    c_recv,
    own,
    scaled,
    d_send,
    d_recv,
    d_own,
    sq_send,
    sq_recv,
    gain,
    local_sem,
    weight_sem,
    draft_sem,
    q_sems,
    t_sems,
    b_sems,
    s_sems,
    c_sems,
    d_sems,
    sq_sems,
):
    me = lax.axis_index("tensor")
    rows, width = q_ref.shape
    slots, kv_heads, _, page, hd = cache.shape
    requests = lengths_ref.shape[0]
    nodes = rows // requests
    per = requests // chunks
    span = per * nodes
    heads = width // hd
    gh = min(groups, heads)
    kv_dev = heads // gh
    pages = table_ref.shape[1] // n
    block = pages * page
    tree_rows = tree_ref.shape[0]
    tree_width = kv_dev * hd
    out_width = draft.shape[2]
    scale = 1.0 / math.sqrt(hd)
    lanes = gh * nodes
    f32, bf16 = jnp.float32, jnp.bfloat16

    relay = n == 4
    part_rows = span // 2
    part_units = b_send.shape[2] // 2

    def flipped(k):
        low = lax.rem(me + k, 2)
        return 2 * lax.rem(me // 2 + k // 2, 2) + low

    def ahead(k):
        return flipped(k) if relay else lax.rem(me + k, n)

    def behind(k):
        return flipped(k) if relay else lax.rem(me + n - k, n)

    def back(k):
        return k if relay else n - k

    def remote(src, dst, sems, index, k):
        return pltpu.make_async_remote_copy(
            src_ref=src,
            dst_ref=dst,
            send_sem=sems.at[(0, *index)],
            recv_sem=sems.at[(1, *index)],
            device_id={"tensor": ahead(k)},
            device_id_type=MESH,
        )

    def send_q(c, k):
        return remote(q_all.at[c, 0], q_all.at[c, k], q_sems, (c, k), k)

    def forward_q(c, i):
        rows_at = pl.ds(i * part_rows, part_rows)
        return remote(
            q_all.at[c, 1 + i, rows_at],
            q_all.at[c, 3, rows_at],
            q_sems,
            (c, 3 - 3 * i),
            2 - i,
        )

    def pass_c(c, i):
        rows_at = pl.ds(i * part_rows, part_rows)
        return remote(
            c_send.at[c, 3, rows_at], c_recv.at[c, 3, rows_at], c_sems, (c, 3 - 3 * i), 1 + i
        )

    def pass_b(c, i):
        at = pl.ds(i * part_units, part_units)
        return remote(
            b_send.at[c, 3, at], b_recv.at[c, 3, at], b_sems, (c, 3 - 3 * i), 1 + i
        )

    def pass_s(c, i):
        return remote(s_send.at[c, 3], s_recv.at[c, 3 - 3 * i], s_sems, (c, 3 - 3 * i), 1 + i)

    def send_t(k):
        at = pl.ds(pl.multiple_of(me * tree_rows, tree_rows), tree_rows)
        return remote(t_send.at[k], t_all.at[:, at, :], t_sems, (k,), k)

    def send_b(c, k):
        return remote(b_send.at[c, back(k)], b_recv.at[c, k], b_sems, (c, k), k)

    def send_s(c, k):
        return remote(s_send.at[c, back(k)], s_recv.at[c, k], s_sems, (c, k), k)

    def send_c(c, k):
        return remote(c_send.at[c, k], c_recv.at[c, k], c_sems, (c, k), k)

    def send_d(c, k):
        return remote(d_send.at[c, k], d_recv.at[c, k], d_sems, (c, k), k)

    def send_sq(c, k):
        return remote(sq_send.at[c], sq_recv.at[c, k], sq_sems, (c, k), k)

    def load_weight(k):
        at = pl.ds(pl.multiple_of(ahead(k) * width, width), width)
        return pltpu.make_async_copy(weight_hbm.at[:, at], weight.at[k], weight_sem.at[k])

    def load_draft(k):
        at = pl.ds(pl.multiple_of(ahead(k) * out_width, out_width), out_width)
        return pltpu.make_async_copy(draft_hbm.at[:, at], draft.at[k], draft_sem.at[k])

    load_cache = pltpu.make_async_copy(codes_hbm, cache, local_sem)
    load_cache.start()
    gain[...] = gain_ref[...].astype(f32)

    barrier = pltpu.get_barrier_semaphore()
    for k in range(1, n):
        pl.semaphore_signal(
            barrier, inc=1, device_id={"tensor": ahead(k)}, device_id_type=MESH
        )
    for c in range(chunks):
        q_all[c, 0] = q_ref[c * span : (c + 1) * span, :]
    for k in range(n):
        first = ahead(k) * heads // groups
        for part in range(2):
            at = pl.ds(pl.multiple_of((part * kv_heads + first) * hd, hd), tree_width)
            t_send[k, part] = tree_ref[:, at].astype(t_send.dtype)
    mine = pl.ds(pl.multiple_of(me * tree_rows, tree_rows), tree_rows)
    t_all[:, mine, :] = t_send[0]
    pl.semaphore_wait(barrier, n - 1)

    near = range(1, 3 if relay else n)
    for k in near:
        send_q(0, k).start()
    for k in range(n):
        load_weight(k).start()
    for k in range(n):
        load_draft(k).start()

    load_cache.wait()

    @pl.loop(0, slots)
    def _(slot):
        for g in range(0, kv_heads, 2):
            codes, results = cache[slot, g : g + 2].astype(f32), []
            for i in range(2):
                level = jnp.full((1, hd), jnp.left_shift(jnp.int32(1), bits_ref[g + i]), jnp.int32)
                level = level.astype(f32)
                ratio = scales_ref[slot, g + i] / level
                for part in range(2):
                    centred = 2.0 * codes[i, part] - (level - 1.0)
                    results.append((ratio[part : part + 1] * centred).astype(bf16))
            for i, result in enumerate(results):
                cache[slot, g + i // 2, i % 2] = result

    for c in range(1, chunks):
        for k in near:
            send_q(c, k).start()
    for k in range(1, n):
        send_t(k).start()

    place = lax.broadcasted_iota(jnp.int32, (block, lanes), 0)

    def stack(c, k, r, j):
        at = slice(r * nodes, (r + 1) * nodes)
        cols = [slice((j * gh + h) * hd, (j * gh + h + 1) * hd) for h in range(gh)]
        return jnp.concatenate([q_all[c, k, at, col] for col in cols], axis=0)

    def receive_q(c):
        for k in (1, 2):
            send_q(c, k).wait_recv()
        for i in range(2):
            forward_q(c, i).start()

    def merge(c):
        for i in range(2):
            pass_b(c, i).wait_recv()
            pass_s(c, i).wait_recv()
            k = 2 - i
            for u in range(i * part_units, (i + 1) * part_units):
                row, below = slice(2 * u, 2 * u + 1), slice(2 * u + 1, 2 * u + 2)
                tops = s_send[c, k, row], s_recv[c, 3 - 3 * i, row]
                overall = jnp.maximum(*tops)
                first = jnp.exp(tops[0] - overall) * s_send[c, k, below]
                other = jnp.exp(tops[1] - overall) * s_recv[c, 3 - 3 * i, below]
                total = first + other
                inverse = 1.0 / jnp.where(total > 0, total, 1.0)
                mixed = (first * inverse) * b_send[c, k, u].astype(f32)
                mixed = mixed + (other * inverse) * b_recv[c, 3, u].astype(f32)
                b_send[c, k, u] = mixed.astype(bf16)
                s_send[c, k, row] = overall
                s_send[c, k, below] = total
            send_b(c, k).start()
            send_s(c, k).start()

    @pl.loop(0, chunks * n)
    def _(step):
        later = jnp.maximum(step - chunks, 0)
        own_step = step < chunks
        c = jnp.where(own_step, step, later // (n - 1))
        k = jnp.where(own_step, 0, 1 + lax.rem(later, n - 1))

        if n > 0:
            if relay:
                @pl.when(step == 1)
                def _():
                    receive_q(0)

                @pl.when((k == 2) & (c < chunks - 1))
                def _():
                    receive_q(c + 1)

                @pl.when(k == 3)
                def _():
                    @pl.when(c > 0)
                    def _():
                        merge(c - 1)

                    for i in range(2):
                        forward_q(c, i).wait_recv()
            else:
                @pl.when(k > 0)
                def _():
                    send_q(c, k).wait_recv()

            first = behind(k) * heads // groups
            for r in range(per):
                request = c * per + r
                ids = [table_ref[request, me * pages + p] for p in range(pages)]
                live = place < lengths_ref[request] - me * block
                for j in range(kv_dev):
                    u = r * kv_dev + j
                    keys, values = (
                        jnp.concatenate([cache[i, first + j, part] for i in ids], axis=0)
                        for part in range(2)
                    )
                    top, total, mixed = attend(stack(c, k, r, j), keys, values, live, scale)
                    s_send[c, k, 2 * u : 2 * u + 1, :] = top
                    s_send[c, k, 2 * u + 1 : 2 * u + 2, :] = total
                    b_send[c, k, u] = mixed.astype(bf16)

            if relay:
                @pl.when(k == 3)
                def _():
                    for i in range(2):
                        pass_b(c, i).start()
                        pass_s(c, i).start()
            else:
                @pl.when(k > 0)
                def _():
                    send_b(c, back(k)).start()
                    send_s(c, back(k)).start()

    for k in range(1, n):
        send_t(k).wait_recv()

    turn_row = lax.broadcasted_iota(jnp.int32, (nodes, lanes), 0)
    turn_lane = lax.broadcasted_iota(jnp.int32, (nodes, lanes), 1)
    turn = (turn_row == lax.rem(turn_lane, nodes)).astype(f32).astype(bf16)

    @pl.loop(0, chunks)
    def _(c):
        for r in range(per):
            request = c * per + r
            turned = lax.dot_general(
                mask_ref[request].astype(f32).astype(bf16),
                turn,
                (((0,), (0,)), ((), ())),
                preferred_element_type=f32,
            )
            at = pl.ds(pl.multiple_of(request * nodes, nodes), nodes)
            for j in range(kv_dev):
                u = r * kv_dev + j
                col = slice(j * hd, (j + 1) * hd)
                keys, values = (t_all[part, at, col].astype(bf16) for part in range(2))
                top, total, mixed = attend(stack(c, 0, r, j), keys, values, turned > 0.5, scale)
                t_stat[c, 2 * u : 2 * u + 1, :] = top
                t_stat[c, 2 * u + 1 : 2 * u + 2, :] = total
                t_out[c, u] = mixed

    if relay:
        merge(chunks - 1)

    for k in range(n):
        load_weight(k).wait()

    tile = min(width, 1024)

    @pl.loop(0, chunks)
    def _(c):
        for k in near:
            send_b(c, k).wait_recv()
            send_s(c, k).wait_recv()
        for u in range(per * kv_dev):
            tops, totals = (
                [t_stat[c, row], s_send[c, 0, row]] + [s_recv[c, k, row] for k in near]
                for row in (slice(2 * u, 2 * u + 1), slice(2 * u + 1, 2 * u + 2))
            )
            overall = functools.reduce(jnp.maximum, tops)
            shares = [jnp.exp(one - overall) * total for one, total in zip(tops, totals)]
            inverse = 1.0 / functools.reduce(jnp.add, shares)
            blocks = [t_out[c, u], b_send[c, 0, u].astype(f32)]
            blocks += [b_recv[c, k, u].astype(f32) for k in near]
            mixed = functools.reduce(
                jnp.add, [one * inverse * b for one, b in zip(shares, blocks)]
            )
            mixed = mixed.T.astype(bf16)
            r, j = u // kv_dev, u % kv_dev
            for h in range(gh):
                attended[
                    r * nodes : (r + 1) * nodes,
                    (j * gh + h) * hd : (j * gh + h + 1) * hd,
                ] = mixed[h * nodes : (h + 1) * nodes]

        def project(k, store):
            @pl.loop(0, width // tile)
            def _(j):
                cols = pl.ds(pl.multiple_of(j * tile, tile), tile)
                store(
                    cols,
                    jnp.dot(attended[...], weight[k, :, cols], preferred_element_type=f32),
                )

        def store_own(cols, product):
            own[c, :, cols] = product

        def store_send(k, cols, product):
            c_send[c, k, :, cols] = product.astype(bf16)

        def store_joined(k, cols, product):
            i = 2 - k
            lower = slice(i * part_rows, (i + 1) * part_rows)
            upper = slice((1 - i) * part_rows, (2 - i) * part_rows)
            passed = c_recv[c, 3, lower, cols].astype(f32)
            c_send[c, k, lower, cols] = (product[lower] + passed).astype(bf16)
            c_send[c, k, upper, cols] = product[upper].astype(bf16)

        if relay:
            project(3, functools.partial(store_send, 3))
            for i in range(2):
                pass_c(c, i).start()
            project(0, store_own)
            for k in (1, 2):
                pass_c(c, 2 - k).wait_recv()
                project(k, functools.partial(store_joined, k))
                send_c(c, k).start()
        else:
            @pl.loop(1, n)
            def _(k):
                project(k, functools.partial(store_send, k))
                send_c(c, k).start()

            project(0, store_own)

    for k in range(n):
        load_draft(k).wait()

    row_of = lax.broadcasted_iota(jnp.int32, (span, 128), 0)
    lane_of = lax.broadcasted_iota(jnp.int32, (span, 128), 1)
    diagonal = row_of == lane_of

    @pl.loop(0, chunks)
    def _(c):
        for k in near:
            send_c(c, k).wait_recv()
        at = pl.ds(pl.multiple_of(c * span, span), span)

        def finish(j, squares):
            cols = pl.ds(pl.multiple_of(j * 128, 128), 128)
            total = own[c, :, cols]
            for k in near:
                total = total + c_recv[c, k, :, cols].astype(f32)
            feature = (residual_ref[at, cols].astype(f32) + total).astype(bf16)
            feature_ref[at, cols] = feature
            feature = feature.astype(f32)
            scaled[:, cols] = (feature * gain[pl.ds(j, 1), :]).astype(bf16)
            return squares + feature * feature

        squares = lax.fori_loop(0, width // 128, finish, jnp.zeros((span, 128), f32))
        column = jnp.sum(squares, axis=1, keepdims=True)
        line = jnp.sum(jnp.where(diagonal, column, 0.0), axis=0, keepdims=True)
        sq_send[c] = jnp.broadcast_to(line, (8, 128))
        for k in range(1, n):
            send_sq(c, k).start()

        @pl.loop(1, n)
        def _(k):
            d_send[c, k] = jnp.dot(
                scaled[...], draft[k], preferred_element_type=f32
            ).astype(bf16)
            send_d(c, k).start()

        d_own[c] = jnp.dot(scaled[...], draft[0], preferred_element_type=f32)

    @pl.loop(0, chunks)
    def _(c):
        for k in range(1, n):
            send_sq(c, k).wait_recv()
            send_d(c, k).wait_recv()
        total = d_own[c]
        line = sq_send[c, 0:1, :]
        for k in range(1, n):
            total = total + d_recv[c, k].astype(f32)
            line = line + sq_recv[c, k, 0:1, :]
        column = jnp.sum(jnp.where(diagonal, line, 0.0), axis=1, keepdims=True)
        inverse = lax.rsqrt(column / (width * n) + epsilon)
        drafted = (total * inverse).astype(bf16)
        source = lax.broadcasted_iota(jnp.int32, (nodes, nodes), 0)
        for r in range(per):
            request = c * per + r
            chosen = (source == parents_ref[pl.ds(request, 1), :]).astype(f32).astype(bf16)
            moved = lax.dot_general(
                chosen,
                drafted[r * nodes : (r + 1) * nodes],
                (((0,), (0,)), ((), ())),
                preferred_element_type=f32,
            )
            to = pl.ds(pl.multiple_of(request * nodes, nodes), nodes)
            drafted_ref[to, :] = moved.astype(bf16)

    for k in range(1, n):
        send_t(k).wait_send()
        for c in range(chunks):
            for send in (send_d, send_sq):
                send(c, k).wait_send()
    for c in range(chunks):
        for k in near:
            for send in (send_q, send_b, send_s, send_c):
                send(c, k).wait_send()
        if relay:
            for i in range(2):
                forward_q(c, i).wait_send()
                pass_b(c, i).wait_send()
                pass_s(c, i).wait_send()
                pass_c(c, i).wait_send()


def hand_over(feature_ref, drafted_ref, feature_out, drafted_out):
    feature_out[...] = feature_ref[...]
    drafted_out[...] = drafted_ref[...]


def shards(
    n,
    query_heads,
    queries,
    tree_states,
    cache_codes,
    cache_scales,
    bit_widths,
    page_table,
    lengths,
    parents,
    tree_mask,
    output_weight,
    residual,
    norm_gain,
    draft_weight,
):
    rows, width = queries.shape
    slots, kv_heads, _, page, hd = cache_codes.shape
    requests = lengths.shape[0]
    nodes = rows // requests
    groups = query_heads // kv_heads
    heads = width // hd
    chunks = 2 if requests % 2 == 0 else 1
    while requests // chunks * nodes > 128:
        chunks *= 2
    span = rows // chunks
    kv_dev = max(1, heads // groups)
    units = requests // chunks * kv_dev
    lanes = min(groups, heads) * nodes
    stat_rows = -(-2 * units // 8) * 8
    tree_rows = tree_states.shape[0]
    wire = jnp.bfloat16 if tree_rows % 16 == 0 else jnp.float32
    out_width = draft_weight.shape[1] // n
    f32, bf16 = jnp.float32, jnp.bfloat16
    dma = pltpu.SemaphoreType.DMA
    vmem, smem, hbm = (
        pl.BlockSpec(memory_space=space) for space in (pltpu.VMEM, pltpu.SMEM, pl.ANY)
    )
    sems = dma((2, chunks, n))
    results = pl.pallas_call(
        functools.partial(kernel, n, chunks, groups),
        out_shape=(
            jax.ShapeDtypeStruct((rows, width), bf16),
            jax.ShapeDtypeStruct((rows, out_width), bf16),
        ),
        in_specs=[vmem, vmem, vmem, smem, smem, smem, vmem, vmem, vmem, vmem, hbm, hbm, hbm],
        out_specs=(vmem, vmem),
        scratch_shapes=[
            pltpu.VMEM(cache_codes.shape, bf16),
            pltpu.VMEM((n, width, width), bf16),
            pltpu.VMEM((n, width, out_width), bf16),
            pltpu.VMEM((chunks, n, span, width), bf16),
            pltpu.VMEM((n, 2, tree_rows, kv_dev * hd), wire),
            pltpu.VMEM((2, rows, kv_dev * hd), wire),
            pltpu.VMEM((chunks, n, units, hd, lanes), bf16),
            pltpu.VMEM((chunks, n, units, hd, lanes), bf16),
            pltpu.VMEM((chunks, n, stat_rows, lanes), f32),
            pltpu.VMEM((chunks, n, stat_rows, lanes), f32),
            pltpu.VMEM((chunks, units, hd, lanes), f32),
            pltpu.VMEM((chunks, stat_rows, lanes), f32),
            pltpu.VMEM((span, width), bf16),
            pltpu.VMEM((chunks, n, span, width), bf16),
            pltpu.VMEM((chunks, n, span, width), bf16),
            pltpu.VMEM((chunks, span, width), f32),
            pltpu.VMEM((span, width), bf16),
            pltpu.VMEM((chunks, n, span, out_width), bf16),
            pltpu.VMEM((chunks, n, span, out_width), bf16),
            pltpu.VMEM((chunks, span, out_width), f32),
            pltpu.VMEM((chunks, 8, 128), f32),
            pltpu.VMEM((chunks, n, 8, 128), f32),
            pltpu.VMEM((width // 128, 128), f32),
            dma,
            dma((n,)),
            dma((n,)),
            sems,
            dma((2, n)),
            sems,
            sems,
            sems,
            sems,
            sems,
        ],
        compiler_params=pltpu.CompilerParams(
            collective_id=0, has_side_effects=True, vmem_limit_bytes=63 * 1024 * 1024
        ),
    )(
        queries,
        tree_states,
        cache_scales,
        bit_widths,
        page_table,
        lengths,
        parents,
        tree_mask,
        residual,
        norm_gain.reshape(-1, 128),
        cache_codes,
        output_weight,
        draft_weight,
    )
    return pl.pallas_call(
        hand_over,
        out_shape=tuple(jax.ShapeDtypeStruct(one.shape, one.dtype) for one in results),
        in_specs=[vmem, vmem],
        out_specs=(vmem, vmem),
        compiler_params=pltpu.CompilerParams(vmem_limit_bytes=63 * 1024 * 1024),
    )(*results)


def solution(mesh):
    n = mesh.shape["tensor"]
    placed = (
        P("dp", "tensor"),
        P(("dp", "tensor"), None),
        P(("dp", "tensor"), None, None, None, None),
        P(("dp", "tensor"), None, None, None),
        P("dp"),
        P("dp", None),
        P("dp"),
        P("dp", None),
        P("dp", None, None),
        P("tensor", None),
        P("dp", "tensor"),
        P("tensor"),
        P("tensor", None),
    )

    def run(*arrays):
        query_heads = arrays[0].shape[1] // arrays[2].shape[-1]
        return jax.shard_map(
            functools.partial(shards, n, query_heads),
            mesh=mesh,
            in_specs=placed,
            out_specs=(P("dp", "tensor"), P("dp", "tensor")),
            check_vma=False,
        )(*arrays)

    return run
```
